512 devices in a mesh: dp: 64 (over z, x), tensor: 8 (over y, core).
Axes of the slice: x: 4, y: 4, z: 16, core: 2. Of those that a mesh axis runs over, the one named last changes fastest.
Arguments:
- queries: bfloat16 [16384, 5120], P('dp', 'tensor'), may hold values from -6 to 6
- branch_keys: bfloat16 [16384, 1024], P('dp', 'tensor'), may hold values from -6 to 6
- branch_values: bfloat16 [16384, 1024], P('dp', 'tensor'), may hold values from -6 to 6
- shared_keys: bfloat16 [4096, 1024], P('dp', 'tensor'), may hold values from -6 to 6
- shared_values: bfloat16 [4096, 1024], P('dp', 'tensor'), may hold values from -6 to 6
- ancestry: int32 [64, 64], replicated, may hold values from 0 to 1, as said below
- plan: int32 [2048], replicated, may hold values from 0 to 63, as said below
Outputs:
- attended: bfloat16 [2048, 8, 5120], P('dp', 'tensor')
The draws below stay inside these ranges and needn't reach their ends.
Inputs may be any that keep to these rules, and one draw needn't show every extreme that they name: ancestry[b, s] is 1 where shared block s is an ancestor of branch b. Every branch has 6 or more and at most 12 ancestor blocks; in every draw some branch has exactly 12. Unit u = 32 * d + j lies on index d of dp and goes to plan[u]. For each j the units j of all indices go to different indices, so every index receives exactly one unit j. Each index sends to 32 indices exactly 1 units each.
All inputs are finite; a program needn't handle non-finite values.
Results may differ from the reference program's by a relative error of at most 0.015.
Values may be sent and summed in bfloat16 or wider, within the bound.
A program may use at most 128 MiB of HBM per device.

```python
import math
import jax
import jax.numpy as jnp
from jax import lax

HEADS = 40
KV_HEADS = 8
HEAD_DIM = 128
STEP = 256
BLOCK = 64
UNIT = 8
BRANCHES = 64
TOKENS = 16384
UNITS_DEV = 32
UNITS = 2048
CAP = 1
SHARED = 64
NODE_BLOCKS = 4
NODES = 8
NPROMPT = 4
PROMPT_BLOCKS = 8
N_DP = 64


def drawn_pair(key):
    query_cols = HEADS * HEAD_DIM
    key_cols = KV_HEADS * HEAD_DIM
    first_key, second_key = jax.random.split(jax.random.fold_in(key, 7), 2)
    query_draw = jnp.clip(jax.random.normal(first_key, (TOKENS, query_cols), jnp.float32), -6.0, 6.0)
    key_draw = jnp.clip(jax.random.normal(second_key, (TOKENS, key_cols), jnp.float32), -6.0, 6.0)
    return (query_draw, key_draw)


def draw_queries(key, part):
    query_draw, key_draw = drawn_pair(key)
    return query_draw.astype(jnp.bfloat16)


def draw_branch_keys(key, part):
    query_draw, key_draw = drawn_pair(key)
    return key_draw.astype(jnp.bfloat16)


def draw_shared_keys(key, part):
    key_cols = KV_HEADS * HEAD_DIM
    shared_rows = SHARED * BLOCK
    base_key = jax.random.fold_in(key, 13)
    result = jnp.clip(jax.random.normal(base_key, (shared_rows, key_cols), jnp.float32), -6.0, 6.0)
    return result.astype(jnp.bfloat16)


def draw_ancestry(key, part):
    keys = jax.random.split(jax.random.fold_in(key, 3), 4)
    prompt_lengths = jax.random.randint(keys[0], (NPROMPT,), 2, PROMPT_BLOCKS + 1)
    prompt_lengths = prompt_lengths.at[0].set(PROMPT_BLOCKS)
    base_node = jnp.arange(BRANCHES, dtype=jnp.int32) * NODES // BRANCHES
    jitter = jax.random.randint(keys[1], (BRANCHES,), -1, 2)
    jitter = jitter.at[0].set(0)
    node_of_branch = (base_node + jitter) % NODES
    prompt_of_node = jax.random.randint(keys[2], (NODES,), 0, NPROMPT)
    prompt_of_node = prompt_of_node.at[0].set(0)
    prompt_of_branch = prompt_of_node[node_of_branch]
    length_of_branch = prompt_lengths[prompt_of_branch]
    block_ids = jnp.arange(SHARED, dtype=jnp.int32)
    prompt_region = NPROMPT * PROMPT_BLOCKS
    in_prompt = block_ids < prompt_region
    prompt_index = block_ids // PROMPT_BLOCKS
    prompt_offset = block_ids % PROMPT_BLOCKS
    node_index = (block_ids - prompt_region) // NODE_BLOCKS
    prompt_part = (prompt_index[None, :] == prompt_of_branch[:, None]) & (prompt_offset[None, :] < length_of_branch[:, None])
    node_part = node_index[None, :] == node_of_branch[:, None]
    canonical = jnp.where(in_prompt[None, :], prompt_part, node_part)
    placement = jax.random.permutation(keys[3], SHARED)
    return canonical[:, placement].astype(jnp.int32)


def draw_plan(key, part):
    first_key, second_key = jax.random.split(jax.random.fold_in(key, 5), 2)
    device_order = jax.random.permutation(first_key, N_DP)
    device_rank = jnp.argsort(device_order)
    offsets = jax.random.permutation(second_key, N_DP)[:UNITS_DEV // CAP]
    slot_ids = jnp.arange(UNITS_DEV, dtype=jnp.int32)
    target = device_order[(device_rank[:, None] + offsets[slot_ids // CAP][None, :]) % N_DP]
    return target.reshape(UNITS).astype(jnp.int32)


def shard_levels(key, shape, pieces, low, largest):
    def one(dim, shards_of):
        steps = jax.random.uniform(jax.random.fold_in(jax.random.fold_in(key, 6), dim), (shards_of,), jnp.float32, low / len(pieces), largest / len(pieces))
        return jnp.repeat(jnp.exp(steps), shape[dim] // shards_of).reshape((-1,) + (1,) * (len(shape) - dim - 1))

    loudness = one(*pieces[0])
    for cut in pieces[1:]:
        loudness = loudness * one(*cut)
    return loudness


def gaussian(stream_key, shape, spread, most, pieces=(), held_as=jnp.bfloat16):
    loudness = shard_levels(stream_key, shape, pieces, -0.22, 0.18) if pieces else 1.0
    array = jax.random.normal(stream_key, shape, jnp.float32) * spread * loudness
    return jnp.minimum(jnp.maximum(array, -most), most).astype(held_as)


def setup_inputs(seed: int = 0) -> dict:
    splits = jax.random.split(jax.random.key(seed), 8)
    return {
        "queries": draw_queries(jax.random.fold_in(splits[7], 71), 0),
        "branch_keys": draw_branch_keys(jax.random.fold_in(splits[7], 71), 0),
        "branch_values": gaussian(splits[2], (TOKENS, KV_HEADS * HEAD_DIM), 1.0, 6.0, ((0, 64), (1, 8))),
        "shared_keys": draw_shared_keys(jax.random.fold_in(splits[7], 71), 0),
        "shared_values": gaussian(splits[4], (SHARED * BLOCK, KV_HEADS * HEAD_DIM), 1.0, 6.0, ((0, 64), (1, 8))),
        "ancestry": draw_ancestry(jax.random.fold_in(splits[7], 71), 0),
        "plan": draw_plan(jax.random.fold_in(splits[7], 71), 0),
    }


negative_fill = -1e+30

def reference(queries, branch_keys, branch_values, shared_keys, shared_values, ancestry, plan):
    per_group = HEADS // KV_HEADS
    scale_factor = 1.0 / math.sqrt(HEAD_DIM)
    width_all = HEADS * HEAD_DIM
    shared_rows = SHARED * BLOCK
    highest = lax.Precision.HIGHEST
    key_table = shared_keys.astype(jnp.float32).reshape(shared_rows, KV_HEADS, HEAD_DIM)
    value_table = shared_values.astype(jnp.float32).reshape(shared_rows, KV_HEADS, HEAD_DIM)
    causal_mask = jnp.arange(STEP)[:, None] >= jnp.arange(STEP)[None, :]

    def one_branch(branch):
        start_row = (branch * STEP).astype(jnp.int32)
        query_block = lax.dynamic_slice_in_dim(queries, start_row, STEP, 0).astype(jnp.float32).reshape(STEP, KV_HEADS, per_group, HEAD_DIM)
        own_keys = lax.dynamic_slice_in_dim(branch_keys, start_row, STEP, 0).astype(jnp.float32).reshape(STEP, KV_HEADS, HEAD_DIM)
        own_values = lax.dynamic_slice_in_dim(branch_values, start_row, STEP, 0).astype(jnp.float32).reshape(STEP, KV_HEADS, HEAD_DIM)
        local_scores = jnp.einsum('pghd,qgd->ghpq', query_block, own_keys, precision=highest) * scale_factor
        local_scores = jnp.where(causal_mask, local_scores, negative_fill)
        local_max = lax.optimization_barrier(jnp.max(local_scores, axis=-1))
        local_exp = jnp.where(causal_mask, jnp.exp(local_scores - local_max[..., None]), 0.0)
        local_sum = lax.optimization_barrier(jnp.sum(local_exp, axis=-1))
        local_weights = lax.optimization_barrier(local_exp.astype(jnp.bfloat16)).astype(jnp.float32)
        local_out = jnp.einsum('ghpq,qgd->pghd', local_weights, own_values, precision=highest)
        local_out = local_out / jnp.transpose(local_sum, (2, 0, 1))[..., None]
        local_out = lax.optimization_barrier(local_out.astype(jnp.bfloat16)).astype(jnp.float32)
        ancestor_row = lax.dynamic_index_in_dim(ancestry, branch, 0, keepdims=False)
        allowed = jnp.repeat(ancestor_row, BLOCK) > 0
        shared_scores = jnp.einsum('pghd,rgd->ghpr', query_block, key_table, precision=highest) * scale_factor
        shared_scores = jnp.where(allowed, shared_scores, negative_fill)
        shared_max = lax.optimization_barrier(jnp.max(shared_scores, axis=-1))
        shared_exp = jnp.where(allowed, jnp.exp(shared_scores - shared_max[..., None]), 0.0)
        shared_sum = lax.optimization_barrier(jnp.sum(shared_exp, axis=-1))
        shared_weights = lax.optimization_barrier(shared_exp.astype(jnp.bfloat16)).astype(jnp.float32)
        shared_acc = jnp.einsum('ghpr,rgd->pghd', shared_weights, value_table, precision=highest)
        first_max = jnp.transpose(local_max, (2, 0, 1))
        second_max = jnp.transpose(shared_max, (2, 0, 1))
        first_sum = jnp.transpose(local_sum, (2, 0, 1))
        second_sum = jnp.transpose(shared_sum, (2, 0, 1))
        top_value = jnp.maximum(first_max, second_max)
        first_weight = first_sum * jnp.exp(first_max - top_value)
        second_weight = jnp.exp(second_max - top_value)
        numerator = first_weight[..., None] * local_out + second_weight[..., None] * shared_acc
        merged = numerator / (first_weight + second_weight * second_sum)[..., None]
        return merged.reshape(STEP, width_all).astype(jnp.bfloat16)
    branch_ids = jnp.arange(BRANCHES, dtype=jnp.int32)
    merged_all = lax.map(one_branch, branch_ids)
    unit_rows = merged_all.reshape(UNITS, UNIT, width_all)
    unit_ids = jnp.arange(UNITS, dtype=jnp.int32)
    source_unit = jnp.zeros((UNITS,), jnp.int32).at[plan * UNITS_DEV + unit_ids % UNITS_DEV].set(unit_ids)
    return jnp.take(unit_rows, source_unit, axis=0)
```

```python
import math

import jax
import jax.numpy as jnp
from jax import lax
from jax.experimental import pallas as pl
from jax.experimental.pallas import tpu as pltpu
from jax.sharding import PartitionSpec as P

HEADS = 40
KV_HEADS = 8
HEAD_DIM = 128
STEP = 256
BLOCK = 64
UNIT = 8
UNITS_DEV = STEP // UNIT
SHARED = 64
MOST = 12
N_DP = 64
N_X = 4
N_Z = 16
N_T = 8
PER = HEADS // KV_HEADS
CHUNKS = (1, 2, 2)
N_CH = len(CHUNKS)
KEYS = STEP + MOST * BLOCK
SCALE = math.log2(math.e) / math.sqrt(HEAD_DIM)
FILL = -1e30
MESH = pl.DeviceIdType.MESH
BF = jnp.bfloat16
F32 = jnp.float32


def iota(shape, dim):
    return lax.broadcasted_iota(jnp.int32, shape, dim)


def dot(a, b, contract=((1,), (0,))):
    return lax.dot_general(a, b, (contract, ((), ())), preferred_element_type=F32)


def flag(mask):
    return jnp.where(mask, 1.0, 0.0).astype(BF)


def kernel(q, bk, bv, sk, sv, anc, plan, out, kbuf, vbuf, kcat, vcat, pack, pick, *rest):
    snd, rest = rest[:N_CH], rest[N_CH:]
    rcv, rest = rest[:N_CH], rest[N_CH:]
    tsnd, rest = rest[:N_CH], rest[N_CH:]
    trcv, rest = rest[:N_CH], rest[N_CH:]
    send_k, send_v, got_ka, got_va, got_kb, got_vc, got_kc, got_vb, a_send, a_got, t_send, t_got = rest

    dp = lax.axis_index("dp")
    t = lax.axis_index("tensor")
    z, x = lax.div(dp, N_X), lax.rem(dp, N_X)
    zm, zd = lax.rem(z, 4), lax.div(z, 4)

    def at(dz, dx):
        return lax.rem(z + (dz + N_Z), N_Z) * N_X + lax.rem(x + dx, N_X)

    far = [at(4 * i, 0) for i in (2, 1, 3)]
    near = [at(d, 0) for d in (1, -1, 2, -2)]
    side = [at(0, i) for i in (1, 2, 3)]

    barrier = pltpu.get_barrier_semaphore()
    for peer in far + near + side:
        pl.semaphore_signal(barrier, inc=1, device_id={"dp": peer}, device_id_type=MESH)
    for i in range(1, N_T):
        pl.semaphore_signal(
            barrier, inc=1, device_id={"tensor": lax.rem(t + i, N_T)}, device_id_type=MESH
        )
    pl.semaphore_wait(barrier, len(far) + len(near) + len(side) + N_T - 1)

    def put(src, dst, send, got, peer):
        pltpu.make_async_remote_copy(
            src_ref=src, dst_ref=dst, send_sem=send, recv_sem=got,
            device_id={"dp": peer}, device_id_type=MESH,
        ).start()

    def await_blocks(buf, count, sem):
        view = buf.at[pl.ds(0, count)]
        pltpu.make_async_copy(view, view, sem).wait()

    k_own = x * 16 + zm * 4 + zd
    v_own = zm * 16 + x * 4 + zd
    for peer in far:
        put(sk, kbuf.at[k_own], send_k, got_ka, peer)
    for peer in far:
        put(sv, vbuf.at[v_own], send_v, got_va, peer)
    kbuf[k_own] = sk[...]
    vbuf[v_own] = sv[...]

    def scan(s, carry):
        count, ids = carry
        hit = anc[dp, s] > 0
        ids = tuple(
            jnp.where(jnp.logical_and(hit, count == k), s, ids[k]) for k in range(MOST)
        )
        return count + jnp.where(hit, 1, 0), ids

    zero = jnp.int32(0)
    count, ids = lax.fori_loop(0, SHARED, scan, (zero, (zero,) * MOST))

    rows16 = flag(iota((N_DP, 16), 1) == (iota((N_DP, 16), 0) >> 2))
    spread = dot(rows16, plan[...].astype(F32).astype(BF))
    quarter = (iota((N_DP, 128), 1) >> 5) == (iota((N_DP, 128), 0) & 3)
    fold = flag((iota((128, UNITS_DEV), 0) & 31) == iota((128, UNITS_DEV), 1))
    table = dot(jnp.where(quarter, spread, 0.0).astype(BF), fold)
    widen = flag((iota((UNITS_DEV, STEP), 1) >> 3) == iota((UNITS_DEV, STEP), 0))
    dest = dot(table.astype(BF), widen)
    mine = jnp.sum(jnp.where(iota((N_DP, STEP), 0) == dp, dest, 0.0), axis=0, keepdims=True)
    row_code = mine.astype(jnp.int32) * UNIT + (iota((1, STEP), 1) & 7)
    pack[...] = flag(iota((N_DP * UNIT, STEP), 0) == row_code)
    to_me = flag(table == dp.astype(F32))
    by_row = flag((iota((STEP, UNITS_DEV), 0) & 31) == iota((STEP, UNITS_DEV), 1))
    source = dot(by_row, to_me, ((1,), (1,)))
    widen_dp = flag((iota((N_DP, N_DP * UNIT), 1) >> 3) == iota((N_DP, N_DP * UNIT), 0))
    source = dot(source.astype(BF), widen_dp)
    same_row = (iota((STEP, N_DP * UNIT), 0) >> 5) == (iota((STEP, N_DP * UNIT), 1) & 7)
    pick[...] = jnp.where(same_row, source, 0.0).astype(BF)

    def k_group(g):
        return kbuf.at[pl.ds(x * 16 + g * 4, 4)]

    def k_across(g):
        for peer in side:
            put(k_group(g), k_group(g), send_k, got_kc, peer)

    def to_near(buf, start, send, gots):
        whole = buf.at[pl.ds(start, 4)]
        put(whole, whole, send, gots[0], near[0])
        put(whole, whole, send, gots[1], near[1])
        put(buf.at[pl.ds(start, 2)], buf.at[pl.ds(start, 2)], send, gots[2], near[2])
        put(buf.at[pl.ds(start + 2, 2)], buf.at[pl.ds(start + 2, 2)], send, gots[2], near[3])

    await_blocks(kbuf, 3, got_ka)
    to_near(kbuf, x * 16 + zm * 4, send_k, [got_kb.at[0], got_kb.at[1], got_kb.at[2]])
    await_blocks(vbuf, 3, got_va)
    v_start = zm * 16 + x * 4
    for i in range(3):
        put(vbuf.at[pl.ds(v_start, 4)], vbuf.at[pl.ds(v_start, 4)], send_v, got_vc.at[i], side[i])
    k_across(zm)
    to_near(vbuf, v_start, send_v, [got_vb] * 3)
    kcat[pl.ds(0, STEP), :] = bk[...]
    vcat[pl.ds(0, STEP), :] = bv[...]
    for i, shift in enumerate((3, 1, 2)):
        await_blocks(kbuf, 4, got_kb.at[i])
        k_across(lax.rem(zm + shift, 4))
    for i in range(3):
        await_blocks(vbuf, 4, got_vc.at[i])
        to_near(vbuf, zm * 16 + lax.rem(x + 3 - i, 4) * 4, send_v, [got_vb] * 3)

    await_blocks(kbuf, 48, got_kc)
    for k in range(MOST):
        s = ids[k]
        bx, bz = s & 3, s >> 2
        kcat[pl.ds(STEP + k * BLOCK, BLOCK), :] = kbuf[bx * 16 + (bz & 3) * 4 + (bz >> 2)]
    await_blocks(vbuf, 48, got_vb)
    for k in range(MOST):
        s = ids[k]
        bx, bz = s & 3, s >> 2
        vcat[pl.ds(STEP + k * BLOCK, BLOCK), :] = vbuf[(bz & 3) * 16 + bx * 4 + (bz >> 2)]

    col = iota((1, KEYS), 1)
    bias = jnp.where(col < STEP + count * BLOCK, 0.0, FILL)
    causal = iota((STEP, STEP), 1) <= iota((STEP, STEP), 0)

    head = 0
    for c, heads in enumerate(CHUNKS):
        for h in range(heads):
            qh = q[:, pl.ds(head * HEAD_DIM, HEAD_DIM)]
            head += 1
            scores = dot(qh, kcat[...], ((1,), (1,)))
            local = jnp.where(causal, scores[:, :STEP], FILL)
            shared = scores[:, STEP:] + bias[:, STEP:]
            top = jnp.maximum(
                jnp.max(local, axis=1, keepdims=True), jnp.max(shared, axis=1, keepdims=True)
            )
            local = jnp.exp2((local - top) * SCALE)
            shared = jnp.exp2((shared - top) * SCALE)
            total = jnp.sum(local, axis=1, keepdims=True) + jnp.sum(shared, axis=1, keepdims=True)
            acc = dot(local.astype(BF), vcat[pl.ds(0, STEP), :]) + dot(
                shared.astype(BF), vcat[pl.ds(STEP, MOST * BLOCK), :]
            )
            merged = (acc / total).astype(BF)
            slots = dot(pack[...], merged).astype(BF)
            snd[c][:, :, pl.ds(h * HEAD_DIM, HEAD_DIM)] = slots.reshape(N_DP, UNIT, HEAD_DIM)

        def send_one(i, carry, c=c):
            peer = lax.rem(dp + i, N_DP)
            put(snd[c].at[peer], rcv[c].at[dp], a_send.at[c], a_got.at[c], peer)
            return carry

        lax.fori_loop(1, N_DP, send_one, 0)
        rcv[c][dp] = snd[c][dp]

    for c, heads in enumerate(CHUNKS):
        await_blocks(rcv[c], N_DP - 1, a_got.at[c])
        wide = heads * HEAD_DIM
        rows = dot(pick[...], rcv[c][...].reshape(N_DP * UNIT, wide)).astype(BF)
        tsnd[c][...] = rows.reshape(N_T, UNITS_DEV, wide)
        for i in range(1, N_T):
            peer = lax.rem(t + i, N_T)
            pltpu.make_async_remote_copy(
                src_ref=tsnd[c].at[peer], dst_ref=trcv[c].at[t],
                send_sem=t_send.at[c], recv_sem=t_got.at[c],
                device_id={"tensor": peer}, device_id_type=MESH,
            ).start()
        trcv[c][t] = tsnd[c][t]

    start = 0
    for c, heads in enumerate(CHUNKS):
        await_blocks(trcv[c], N_T - 1, t_got.at[c])
        wide = heads * HEAD_DIM
        for peer in range(N_T):
            out[:, pl.ds(peer * PER * HEAD_DIM + start, wide)] = trcv[c][peer]
        start += wide

    await_blocks(kbuf, 63, send_k)
    await_blocks(vbuf, 63, send_v)
    for c in range(N_CH):
        await_blocks(snd[c], N_DP - 1, a_send.at[c])
        await_blocks(tsnd[c], N_T - 1, t_send.at[c])


def body(queries, branch_keys, branch_values, shared_keys, shared_values, ancestry, plan):
    vmem = pl.BlockSpec(memory_space=pltpu.VMEM)
    smem = pl.BlockSpec(memory_space=pltpu.SMEM)
    widths = [heads * HEAD_DIM for heads in CHUNKS]
    dma = pltpu.SemaphoreType.DMA
    rows = pl.pallas_call(
        kernel,
        name="tree_step",
        out_shape=jax.ShapeDtypeStruct((UNITS_DEV, HEADS * HEAD_DIM), BF),
        in_specs=[vmem] * 5 + [smem, vmem],
        out_specs=vmem,
        scratch_shapes=[
            pltpu.VMEM((SHARED, BLOCK, HEAD_DIM), BF),
            pltpu.VMEM((SHARED, BLOCK, HEAD_DIM), BF),
            pltpu.VMEM((KEYS, HEAD_DIM), BF),
            pltpu.VMEM((KEYS, HEAD_DIM), BF),
            pltpu.VMEM((N_DP * UNIT, STEP), BF),
            pltpu.VMEM((STEP, N_DP * UNIT), BF),
            *[pltpu.VMEM((N_DP, UNIT, w), BF) for w in widths],
            *[pltpu.VMEM((N_DP, UNIT, w), BF) for w in widths],
            *[pltpu.VMEM((N_T, UNITS_DEV, w), BF) for w in widths],
            *[pltpu.VMEM((N_T, UNITS_DEV, w), BF) for w in widths],
            dma, dma, dma, dma, dma((3,)), dma((3,)), dma, dma,
            dma((N_CH,)), dma((N_CH,)), dma((N_CH,)), dma((N_CH,)),
        ],
        compiler_params=pltpu.CompilerParams(
            collective_id=0, has_side_effects=True, vmem_limit_bytes=40 << 20
        ),
    )(
        queries, branch_keys, branch_values, shared_keys, shared_values, ancestry,
        plan.reshape(16, 128),
    )
    return rows.reshape(UNITS_DEV, 1, HEADS * HEAD_DIM)


def solution(mesh):
    return jax.shard_map(
        body,
        mesh=mesh,
        in_specs=(
            P("dp", "tensor"),
            P("dp", "tensor"),
            P("dp", "tensor"),
            P("dp", "tensor"),
            P("dp", "tensor"),
            P(),
            P(),
        ),
        out_specs=P("dp", "tensor", None),
        check_vma=False,
    )
```

```python
import math

import jax
import jax.numpy as jnp
from jax import lax
from jax.experimental import pallas as pl
from jax.experimental.pallas import tpu as pltpu
from jax.sharding import PartitionSpec as P

HEADS = 40
KV_HEADS = 8
HEAD_DIM = 128
STEP = 256
BLOCK = 64
UNIT = 8
UNITS_DEV = STEP // UNIT
SHARED = 64
MOST = 12
N_DP = 64
N_X = 4
N_Z = 16
N_T = 8
PER = HEADS // KV_HEADS
CHUNKS = (1, 2, 2)
N_CH = len(CHUNKS)
KEYS = STEP + MOST * BLOCK
SCALE = math.log2(math.e) / math.sqrt(HEAD_DIM)
FILL = -1e30
MESH = pl.DeviceIdType.MESH
BF = jnp.bfloat16
F32 = jnp.float32


def iota(shape, dim):
    return lax.broadcasted_iota(jnp.int32, shape, dim)


def dot(a, b, contract=((1,), (0,))):
    return lax.dot_general(a, b, (contract, ((), ())), preferred_element_type=F32)


def flag(mask):
    return jnp.where(mask, 1.0, 0.0).astype(BF)


def kernel(
    q_in, bk_in, bv_in, sk, sv, anc_in, plan_in, out,
    q, anc, plan, kbuf, vbuf, kcat, vcat, pack, pack_row, by_row, pick, *rest
):
    snd, rest = rest[:N_CH], rest[N_CH:]
    rcv, rest = rest[:N_CH], rest[N_CH:]
    tsnd, rest = rest[:N_CH], rest[N_CH:]
    trcv, rest = rest[:N_CH], rest[N_CH:]
    send_k, send_v, got_ka, got_va, got_kb, got_vc, got_kc, got_vb, a_send, a_got, t_send, t_got, load = rest

    dp = lax.axis_index("dp")
    t = lax.axis_index("tensor")
    z, x = lax.div(dp, N_X), lax.rem(dp, N_X)
    zm, zd = lax.rem(z, 4), lax.div(z, 4)

    def at(dz, dx):
        return lax.rem(z + (dz + N_Z), N_Z) * N_X + lax.rem(x + dx, N_X)

    far = [at(4 * i, 0) for i in (2, 1, 3)]
    near = [at(d, 0) for d in (1, -1, 2, -2)]
    side = [at(0, i) for i in (1, 2, 3)]

    k_own = x * 16 + zm * 4 + zd
    v_own = zm * 16 + x * 4 + zd
    loads = [
        pltpu.make_async_copy(src, dst, load.at[i])
        for i, (src, dst) in enumerate((
            (sk, kbuf.at[k_own]), (sv, vbuf.at[v_own]), (anc_in, anc), (plan_in, plan),
            (q_in, q), (bk_in, kcat.at[pl.ds(0, STEP)]), (bv_in, vcat.at[pl.ds(0, STEP)]),
        ))
    ]
    for copy in loads:
        copy.start()

    barrier = pltpu.get_barrier_semaphore()
    for peer in far + near + side:
        pl.semaphore_signal(barrier, inc=1, device_id={"dp": peer}, device_id_type=MESH)
    for i in range(1, N_T):
        pl.semaphore_signal(
            barrier, inc=1, device_id={"tensor": lax.rem(t + i, N_T)}, device_id_type=MESH
        )
    pl.semaphore_wait(barrier, len(far) + len(near) + len(side) + N_T - 1)

    def put(src, dst, send, got, peer):
        pltpu.make_async_remote_copy(
            src_ref=src, dst_ref=dst, send_sem=send, recv_sem=got,
            device_id={"dp": peer}, device_id_type=MESH,
        ).start()

    def await_blocks(buf, count, sem):
        view = buf.at[pl.ds(0, count)]
        pltpu.make_async_copy(view, view, sem).wait()

    loads[0].wait()
    for peer in far:
        put(kbuf.at[k_own], kbuf.at[k_own], send_k, got_ka, peer)
    loads[1].wait()
    for peer in far:
        put(vbuf.at[v_own], vbuf.at[v_own], send_v, got_va, peer)

    for copy in loads[2:]:
        copy.wait()

    def scan(s, carry):
        count, ids = carry
        hit = anc[dp, s] > 0
        ids = tuple(
            jnp.where(jnp.logical_and(hit, count == k), s, ids[k]) for k in range(MOST)
        )
        return count + jnp.where(hit, 1, 0), ids

    zero = jnp.int32(0)
    count, ids = lax.fori_loop(0, SHARED, scan, (zero, (zero,) * MOST))

    rows16 = flag(iota((N_DP, 16), 1) == (iota((N_DP, 16), 0) >> 2))
    spread = dot(rows16, plan[...].astype(F32).astype(BF))
    quarter = (iota((N_DP, 128), 1) >> 5) == (iota((N_DP, 128), 0) & 3)
    fold = flag((iota((128, UNITS_DEV), 0) & 31) == iota((128, UNITS_DEV), 1))
    table = dot(jnp.where(quarter, spread, 0.0).astype(BF), fold)
    widen = flag((iota((UNITS_DEV, STEP), 1) >> 3) == iota((UNITS_DEV, STEP), 0))
    dest = dot(table.astype(BF), widen)
    mine = jnp.sum(jnp.where(iota((N_DP, STEP), 0) == dp, dest, 0.0), axis=0, keepdims=True)
    row_code = mine.astype(jnp.int32) * UNIT + (iota((1, STEP), 1) & 7)
    pack[...] = flag(iota((N_DP * UNIT, STEP), 0) == row_code)
    unit_of = flag((iota((UNITS_DEV, STEP), 1) & 31) == iota((UNITS_DEV, STEP), 0))
    dest = dot(table.astype(BF), unit_of)
    mine = jnp.sum(jnp.where(iota((N_DP, STEP), 0) == dp, dest, 0.0), axis=0, keepdims=True)
    row_code = mine.astype(jnp.int32) * N_T + (iota((1, STEP), 1) >> 5)
    pack_row[...] = flag(iota((N_DP * N_T, STEP), 0) == row_code)
    row, col = iota((STEP, STEP), 0), iota((STEP, STEP), 1)
    by_row[...] = flag((row & 31) * UNIT + (row >> 5) == col)
    to_me = flag(table == dp.astype(F32))
    source = dot(unit_of, to_me, ((0,), (1,)))
    widen_dp = flag((iota((N_DP, N_DP * UNIT), 1) >> 3) == iota((N_DP, N_DP * UNIT), 0))
    source = dot(source.astype(BF), widen_dp)
    same_row = (iota((STEP, N_DP * UNIT), 0) >> 5) == (iota((STEP, N_DP * UNIT), 1) & 7)
    pick[...] = jnp.where(same_row, source, 0.0).astype(BF)

    def k_group(g):
        return kbuf.at[pl.ds(x * 16 + g * 4, 4)]

    def k_across(g):
        for peer in side:
            put(k_group(g), k_group(g), send_k, got_kc, peer)

    def to_near(buf, start, send, gots):
        whole = buf.at[pl.ds(start, 4)]
        put(whole, whole, send, gots[0], near[0])
        put(whole, whole, send, gots[1], near[1])
        put(buf.at[pl.ds(start, 2)], buf.at[pl.ds(start, 2)], send, gots[2], near[2])
        put(buf.at[pl.ds(start + 2, 2)], buf.at[pl.ds(start + 2, 2)], send, gots[2], near[3])

    await_blocks(kbuf, 3, got_ka)
    to_near(kbuf, x * 16 + zm * 4, send_k, [got_kb.at[0], got_kb.at[1], got_kb.at[2]])
    await_blocks(vbuf, 3, got_va)
    v_start = zm * 16 + x * 4
    for i in range(3):
        put(vbuf.at[pl.ds(v_start, 4)], vbuf.at[pl.ds(v_start, 4)], send_v, got_vc.at[i], side[i])
    k_across(zm)
    to_near(vbuf, v_start, send_v, [got_vb] * 3)
    for i, shift in enumerate((3, 1, 2)):
        await_blocks(kbuf, 4, got_kb.at[i])
        k_across(lax.rem(zm + shift, 4))
    for i in range(3):
        await_blocks(vbuf, 4, got_vc.at[i])
        to_near(vbuf, zm * 16 + lax.rem(x + 3 - i, 4) * 4, send_v, [got_vb] * 3)

    await_blocks(kbuf, 48, got_kc)
    for k in range(MOST):
        s = ids[k]
        bx, bz = s & 3, s >> 2
        kcat[pl.ds(STEP + k * BLOCK, BLOCK), :] = kbuf[bx * 16 + (bz & 3) * 4 + (bz >> 2)]
    await_blocks(vbuf, 48, got_vb)
    for k in range(MOST):
        s = ids[k]
        bx, bz = s & 3, s >> 2
        vcat[pl.ds(STEP + k * BLOCK, BLOCK), :] = vbuf[(bz & 3) * 16 + bx * 4 + (bz >> 2)]

    col = iota((1, KEYS), 1)
    bias = jnp.where(col < STEP + count * BLOCK, 0.0, FILL)
    causal = iota((STEP, STEP), 1) <= iota((STEP, STEP), 0)

    def attend(head):
        qh = q[:, pl.ds(head * HEAD_DIM, HEAD_DIM)]
        scores = dot(qh, kcat[...], ((1,), (1,)))
        local = jnp.where(causal, scores[:, :STEP], FILL)
        shared = scores[:, STEP:] + bias[:, STEP:]
        top = jnp.maximum(
            jnp.max(local, axis=1, keepdims=True), jnp.max(shared, axis=1, keepdims=True)
        )
        local = jnp.exp2((local - top) * SCALE)
        shared = jnp.exp2((shared - top) * SCALE)
        total = jnp.sum(local, axis=1, keepdims=True) + jnp.sum(shared, axis=1, keepdims=True)
        acc = dot(local.astype(BF), vcat[pl.ds(0, STEP), :]) + dot(
            shared.astype(BF), vcat[pl.ds(STEP, MOST * BLOCK), :]
        )
        return (acc / total).astype(BF)

    def send_dp(c):
        def send_one(i, carry):
            peer = lax.rem(dp + i, N_DP)
            put(snd[c].at[peer], rcv[c].at[dp], a_send.at[c], a_got.at[c], peer)
            return carry

        lax.fori_loop(1, N_DP, send_one, 0)
        rcv[c][dp] = snd[c][dp]

    def send_tensor(c):
        for i in range(1, N_T):
            peer = lax.rem(t + i, N_T)
            pltpu.make_async_remote_copy(
                src_ref=tsnd[c].at[peer], dst_ref=trcv[c].at[t],
                send_sem=t_send.at[c], recv_sem=t_got.at[c],
                device_id={"tensor": peer}, device_id_type=MESH,
            ).start()
        trcv[c][t] = tsnd[c][t]

    def picked(c):
        await_blocks(rcv[c], N_DP - 1, a_got.at[c])
        slots = rcv[c][...].reshape(N_DP * UNIT, CHUNKS[c] * HEAD_DIM)
        return dot(pick[...], slots).astype(BF)

    last = N_CH - 1
    head = 0
    for c, heads in enumerate(CHUNKS):
        for h in range(heads):
            merged = attend(head)
            head += 1
            place = pl.ds(h * HEAD_DIM, HEAD_DIM)
            if c < last:
                slots = dot(pack[...], merged).astype(BF)
                snd[c][:, :, place] = slots.reshape(N_DP, UNIT, HEAD_DIM)
            else:
                rows = dot(by_row[...], merged).astype(BF)
                tsnd[c][:, :, place] = rows.reshape(N_T, UNITS_DEV, HEAD_DIM)
        if c < last:
            send_dp(c)
        else:
            send_tensor(c)
    await_blocks(trcv[last], N_T - 1, t_got.at[last])
    wide = CHUNKS[last] * HEAD_DIM
    slots = dot(pack_row[...], trcv[last][...].reshape(STEP, wide)).astype(BF)
    snd[last][...] = slots.reshape(N_DP, N_T, wide)
    send_dp(last)

    for c in range(last):
        tsnd[c][...] = picked(c).reshape(N_T, UNITS_DEV, CHUNKS[c] * HEAD_DIM)
        send_tensor(c)
    start = 0
    for c, heads in enumerate(CHUNKS):
        wide = heads * HEAD_DIM
        if c < last:
            await_blocks(trcv[c], N_T - 1, t_got.at[c])
        else:
            rows = picked(c)
        for peer in range(N_T):
            part = trcv[c][peer] if c < last else rows[peer * UNITS_DEV : (peer + 1) * UNITS_DEV]
            out[:, pl.ds(peer * PER * HEAD_DIM + start, wide)] = part
        start += wide

    await_blocks(kbuf, 63, send_k)
    await_blocks(vbuf, 63, send_v)
    for c in range(N_CH):
        await_blocks(snd[c], N_DP - 1, a_send.at[c])
        await_blocks(tsnd[c], N_T - 1, t_send.at[c])


def body(queries, branch_keys, branch_values, shared_keys, shared_values, ancestry, plan):
    vmem = pl.BlockSpec(memory_space=pltpu.VMEM)
    hbm = pl.BlockSpec(memory_space=pltpu.HBM)
    widths = [heads * HEAD_DIM for heads in CHUNKS]
    dma = pltpu.SemaphoreType.DMA
    rows = pl.pallas_call(
        kernel,
        name="tree_step",
        out_shape=pltpu.VMEM((UNITS_DEV, HEADS * HEAD_DIM), BF),
        in_specs=[hbm] * 7,
        out_specs=vmem,
        scratch_shapes=[
            pltpu.VMEM((STEP, PER * HEAD_DIM), BF),
            pltpu.SMEM((N_DP, SHARED), jnp.int32),
            pltpu.VMEM((16, 128), jnp.int32),
            pltpu.VMEM((SHARED, BLOCK, HEAD_DIM), BF),
            pltpu.VMEM((SHARED, BLOCK, HEAD_DIM), BF),
            pltpu.VMEM((KEYS, HEAD_DIM), BF),
            pltpu.VMEM((KEYS, HEAD_DIM), BF),
            pltpu.VMEM((N_DP * UNIT, STEP), BF),
            pltpu.VMEM((N_DP * N_T, STEP), BF),
            pltpu.VMEM((STEP, STEP), BF),
            pltpu.VMEM((STEP, N_DP * UNIT), BF),
            *[pltpu.VMEM((N_DP, UNIT, w), BF) for w in widths],
            *[pltpu.VMEM((N_DP, UNIT, w), BF) for w in widths],
            *[pltpu.VMEM((N_T, UNITS_DEV, w), BF) for w in widths],
            *[pltpu.VMEM((N_T, UNITS_DEV, w), BF) for w in widths],
            dma, dma, dma, dma, dma((3,)), dma((3,)), dma, dma,
            dma((N_CH,)), dma((N_CH,)), dma((N_CH,)), dma((N_CH,)), dma((7,)),
        ],
        compiler_params=pltpu.CompilerParams(
            collective_id=0, has_side_effects=True, vmem_limit_bytes=40 << 20
        ),
    )(
        *[
            pltpu.with_memory_space_constraint(a, pltpu.HBM)
            for a in (
                queries, branch_keys, branch_values, shared_keys, shared_values, ancestry,
                plan.reshape(16, 128),
            )
        ]
    )
    return rows.reshape(UNITS_DEV, 1, HEADS * HEAD_DIM)


def solution(mesh):
    return jax.shard_map(
        body,
        mesh=mesh,
        in_specs=(
            P("dp", "tensor"),
            P("dp", "tensor"),
            P("dp", "tensor"),
            P("dp", "tensor"),
            P("dp", "tensor"),
            P(),
            P(),
        ),
        out_specs=P("dp", "tensor", None),
        check_vma=False,
    )
```

```python
import math

import jax
import jax.numpy as jnp
from jax import lax
from jax.experimental import pallas as pl
from jax.experimental.pallas import tpu as pltpu
from jax.sharding import PartitionSpec as P

HEADS = 40
KV_HEADS = 8
HEAD_DIM = 128
STEP = 256
BLOCK = 64
UNIT = 8
UNITS_DEV = STEP // UNIT
SHARED = 64
MOST = 12
N_DP = 64
N_X = 4
N_Z = 16
N_T = 8
PER = HEADS // KV_HEADS
CHUNKS = (2, 3)
N_CH = len(CHUNKS)
KEYS = STEP + MOST * BLOCK
SCALE = math.log2(math.e) / math.sqrt(HEAD_DIM)
FILL = -1e30
MESH = pl.DeviceIdType.MESH
BF = jnp.bfloat16
F32 = jnp.float32


def iota(shape, dim):
    return lax.broadcasted_iota(jnp.int32, shape, dim)


def dot(a, b, contract=((1,), (0,))):
    return lax.dot_general(a, b, (contract, ((), ())), preferred_element_type=F32)


def flag(mask):
    return jnp.where(mask, 1.0, 0.0).astype(BF)


def kernel(
    q_in, bk_in, bv_in, sk, sv, anc_in, plan_in, out,
    q, anc, plan, kbuf, vbuf, kcat, vcat, pack, pack_row, by_row, pick, *rest
):
    snd, rest = rest[:N_CH], rest[N_CH:]
    rcv, rest = rest[:N_CH], rest[N_CH:]
    tsnd, rest = rest[:N_CH], rest[N_CH:]
    trcv, rest = rest[:N_CH], rest[N_CH:]
    send_k, send_v, got_ka, got_va, got_kb, got_vc, got_kc, got_vb, a_send, a_got, t_send, t_got, load = rest

    dp = lax.axis_index("dp")
    t = lax.axis_index("tensor")
    z, x = dp >> 2, dp & 3
    zm, zd = z & 3, z >> 2

    def at(dz, dx):
        return (((z + dz) & (N_Z - 1)) << 2) + ((x + dx) & (N_X - 1))

    far = [at(4 * i, 0) for i in (2, 1, 3)]
    near = [at(d, 0) for d in (1, -1, 2, -2)]
    side = [at(0, i) for i in (1, 2, 3)]

    k_own = x * 16 + zm * 4 + zd
    v_own = zm * 16 + x * 4 + zd
    loads = [
        pltpu.make_async_copy(src, dst, load.at[i])
        for i, (src, dst) in enumerate((
            (sk, kbuf.at[k_own]), (sv, vbuf.at[v_own]), (anc_in, anc), (plan_in, plan),
            (q_in, q), (bk_in, kcat.at[pl.ds(0, STEP)]), (bv_in, vcat.at[pl.ds(0, STEP)]),
        ))
    ]
    for copy in loads[:2]:
        copy.start()

    barrier = pltpu.get_barrier_semaphore()
    for peer in far + near + side:
        pl.semaphore_signal(barrier, inc=1, device_id=(peer, t), device_id_type=MESH)
    for i in range(1, N_T):
        pl.semaphore_signal(
            barrier, inc=1, device_id=(dp, (t + i) & (N_T - 1)), device_id_type=MESH
        )
    for copy in loads[2:]:
        copy.start()
    pl.semaphore_wait(barrier, len(far) + len(near) + len(side) + N_T - 1)

    def put(src, dst, send, got, peer):
        pltpu.make_async_remote_copy(
            src_ref=src, dst_ref=dst, send_sem=send, recv_sem=got,
            device_id=(peer, t), device_id_type=MESH,
        ).start()

    def await_blocks(buf, count, sem):
        view = buf.at[pl.ds(0, count)]
        pltpu.make_async_copy(view, view, sem).wait()

    loads[0].wait()
    for peer in far:
        put(kbuf.at[k_own], kbuf.at[k_own], send_k, got_ka, peer)
    loads[1].wait()
    for peer in far:
        put(vbuf.at[v_own], vbuf.at[v_own], send_v, got_va, peer)

    for copy in loads[2:]:
        copy.wait()

    def scan(s, carry):
        count, ids = carry
        hit = anc[dp, s] > 0
        ids = tuple(
            jnp.where(jnp.logical_and(hit, count == k), s, ids[k]) for k in range(MOST)
        )
        return count + jnp.where(hit, 1, 0), ids

    zero = jnp.int32(0)
    count, ids = lax.fori_loop(0, SHARED, scan, (zero, (zero,) * MOST))

    rows16 = flag(iota((N_DP, 16), 1) == (iota((N_DP, 16), 0) >> 2))
    spread = dot(rows16, plan[...].astype(F32).astype(BF))
    quarter = (iota((N_DP, 128), 1) >> 5) == (iota((N_DP, 128), 0) & 3)
    fold = flag((iota((128, UNITS_DEV), 0) & 31) == iota((128, UNITS_DEV), 1))
    table = dot(jnp.where(quarter, spread, 0.0).astype(BF), fold)
    widen = flag((iota((UNITS_DEV, STEP), 1) >> 3) == iota((UNITS_DEV, STEP), 0))
    dest = dot(table.astype(BF), widen)
    mine = jnp.sum(jnp.where(iota((N_DP, STEP), 0) == dp, dest, 0.0), axis=0, keepdims=True)
    row_code = mine.astype(jnp.int32) * UNIT + (iota((1, STEP), 1) & 7)
    pack[...] = flag(iota((N_DP * UNIT, STEP), 0) == row_code)
    unit_of = flag((iota((UNITS_DEV, STEP), 1) & 31) == iota((UNITS_DEV, STEP), 0))
    dest = dot(table.astype(BF), unit_of)
    mine = jnp.sum(jnp.where(iota((N_DP, STEP), 0) == dp, dest, 0.0), axis=0, keepdims=True)
    row_code = mine.astype(jnp.int32) * N_T + (iota((1, STEP), 1) >> 5)
    pack_row[...] = flag(iota((N_DP * N_T, STEP), 0) == row_code)
    row, col = iota((STEP, STEP), 0), iota((STEP, STEP), 1)
    by_row[...] = flag((row & 31) * UNIT + (row >> 5) == col)
    to_me = flag(table == dp.astype(F32))
    source = dot(unit_of, to_me, ((0,), (1,)))
    widen_dp = flag((iota((N_DP, N_DP * UNIT), 1) >> 3) == iota((N_DP, N_DP * UNIT), 0))
    source = dot(source.astype(BF), widen_dp)
    same_row = (iota((STEP, N_DP * UNIT), 0) >> 5) == (iota((STEP, N_DP * UNIT), 1) & 7)
    pick[...] = jnp.where(same_row, source, 0.0).astype(BF)

    def k_group(g):
        return kbuf.at[pl.ds(x * 16 + g * 4, 4)]

    def k_across(g):
        for peer in side:
            put(k_group(g), k_group(g), send_k, got_kc, peer)

    def to_near(buf, start, send, gots, way=None):
        whole = buf.at[pl.ds(start, 4)]
        put(whole, whole, send, gots[0], near[0])
        put(whole, whole, send, gots[1], near[1])
        if way is not None:
            put(whole, whole, send, gots[2], near[2 + way])
            return
        put(buf.at[pl.ds(start, 2)], buf.at[pl.ds(start, 2)], send, gots[2], near[2])
        put(buf.at[pl.ds(start + 2, 2)], buf.at[pl.ds(start + 2, 2)], send, gots[2], near[3])

    await_blocks(kbuf, 3, got_ka)
    to_near(kbuf, x * 16 + zm * 4, send_k, [got_kb.at[0], got_kb.at[1], got_kb.at[2]])
    await_blocks(vbuf, 3, got_va)
    v_start = zm * 16 + x * 4
    for i in range(3):
        put(vbuf.at[pl.ds(v_start, 4)], vbuf.at[pl.ds(v_start, 4)], send_v, got_vc.at[i], side[i])
    k_across(zm)
    to_near(vbuf, v_start, send_v, [got_vb] * 3, 0)
    for i, shift in enumerate((3, 1, 2)):
        await_blocks(kbuf, 4, got_kb.at[i])
        k_across((zm + shift) & 3)
    for i in range(3):
        await_blocks(vbuf, 4, got_vc.at[i])
        to_near(vbuf, zm * 16 + ((x + 3 - i) & 3) * 4, send_v, [got_vb] * 3, (i + 1) & 1)

    await_blocks(kbuf, 48, got_kc)
    for k in range(MOST):
        s = ids[k]
        bx, bz = s & 3, s >> 2
        kcat[pl.ds(STEP + k * BLOCK, BLOCK), :] = kbuf[bx * 16 + (bz & 3) * 4 + (bz >> 2)]
    await_blocks(vbuf, 48, got_vb)
    for k in range(MOST):
        s = ids[k]
        bx, bz = s & 3, s >> 2
        vcat[pl.ds(STEP + k * BLOCK, BLOCK), :] = vbuf[(bz & 3) * 16 + bx * 4 + (bz >> 2)]

    col = iota((1, KEYS), 1)
    bias = jnp.where(col < STEP + count * BLOCK, 0.0, FILL)
    causal = iota((STEP, STEP), 1) <= iota((STEP, STEP), 0)

    def attend(head):
        qh = q[:, pl.ds(head * HEAD_DIM, HEAD_DIM)]
        scores = dot(qh, kcat[...], ((1,), (1,)))
        local = jnp.where(causal, scores[:, :STEP], FILL)
        shared = scores[:, STEP:] + bias[:, STEP:]
        top = jnp.maximum(
            jnp.max(local, axis=1, keepdims=True), jnp.max(shared, axis=1, keepdims=True)
        )
        local = jnp.exp2((local - top) * SCALE)
        shared = jnp.exp2((shared - top) * SCALE)
        total = jnp.sum(local, axis=1, keepdims=True) + jnp.sum(shared, axis=1, keepdims=True)
        acc = dot(local.astype(BF), vcat[pl.ds(0, STEP), :]) + dot(
            shared.astype(BF), vcat[pl.ds(STEP, MOST * BLOCK), :]
        )
        return (acc / total).astype(BF)

    def send_dp(c):
        def send_one(i, carry):
            m = i >> 2
            half = (m + 1) >> 1
            pz = jnp.where((m & 1) == 1, half, (N_Z - half) & (N_Z - 1))
            peer = (pz << 2) + ((i + x) & (N_X - 1))

            @pl.when(peer != dp)
            def _():
                put(snd[c].at[peer], rcv[c].at[dp], a_send.at[c], a_got.at[c], peer)

            return carry

        lax.fori_loop(0, N_DP, send_one, 0)
        rcv[c][dp] = snd[c][dp]

    def send_tensor(c):
        for i in range(1, N_T):
            peer = (t + i) & (N_T - 1)
            pltpu.make_async_remote_copy(
                src_ref=tsnd[c].at[peer], dst_ref=trcv[c].at[t],
                send_sem=t_send.at[c], recv_sem=t_got.at[c],
                device_id=(dp, peer), device_id_type=MESH,
            ).start()
        trcv[c][t] = tsnd[c][t]

    def picked(c):
        await_blocks(rcv[c], N_DP - 1, a_got.at[c])
        slots = rcv[c][...].reshape(N_DP * UNIT, CHUNKS[c] * HEAD_DIM)
        return dot(pick[...], slots).astype(BF)

    last = N_CH - 1
    head = 0
    for c, heads in enumerate(CHUNKS):
        for h in range(heads):
            merged = attend(head)
            head += 1
            place = pl.ds(h * HEAD_DIM, HEAD_DIM)
            if c < last:
                slots = dot(pack[...], merged).astype(BF)
                snd[c][:, :, place] = slots.reshape(N_DP, UNIT, HEAD_DIM)
            else:
                rows = dot(by_row[...], merged).astype(BF)
                tsnd[c][:, :, place] = rows.reshape(N_T, UNITS_DEV, HEAD_DIM)
        if c < last:
            send_dp(c)
        else:
            send_tensor(c)
    await_blocks(trcv[last], N_T - 1, t_got.at[last])
    wide = CHUNKS[last] * HEAD_DIM
    slots = dot(pack_row[...], trcv[last][...].reshape(STEP, wide)).astype(BF)
    snd[last][...] = slots.reshape(N_DP, N_T, wide)
    send_dp(last)

    for c in range(last):
        tsnd[c][...] = picked(c).reshape(N_T, UNITS_DEV, CHUNKS[c] * HEAD_DIM)
        send_tensor(c)
    start = 0
    for c, heads in enumerate(CHUNKS):
        wide = heads * HEAD_DIM
        if c < last:
            await_blocks(trcv[c], N_T - 1, t_got.at[c])
        else:
            rows = picked(c)
        for peer in range(N_T):
            part = trcv[c][peer] if c < last else rows[peer * UNITS_DEV : (peer + 1) * UNITS_DEV]
            out[:, pl.ds(peer * PER * HEAD_DIM + start, wide)] = part
        start += wide

    await_blocks(kbuf, 63, send_k)
    await_blocks(vbuf, 63, send_v)
    for c in range(N_CH):
        await_blocks(snd[c], N_DP - 1, a_send.at[c])
        await_blocks(tsnd[c], N_T - 1, t_send.at[c])


def body(queries, branch_keys, branch_values, shared_keys, shared_values, ancestry, plan):
    vmem = pl.BlockSpec(memory_space=pltpu.VMEM)
    hbm = pl.BlockSpec(memory_space=pltpu.HBM)
    widths = [heads * HEAD_DIM for heads in CHUNKS]
    dma = pltpu.SemaphoreType.DMA
    rows = pl.pallas_call(
        kernel,
        name="tree_step",
        out_shape=pltpu.VMEM((UNITS_DEV, HEADS * HEAD_DIM), BF),
        in_specs=[hbm] * 7,
        out_specs=vmem,
        scratch_shapes=[
            pltpu.VMEM((STEP, PER * HEAD_DIM), BF),
            pltpu.SMEM((N_DP, SHARED), jnp.int32),
            pltpu.VMEM((16, 128), jnp.int32),
            pltpu.VMEM((SHARED, BLOCK, HEAD_DIM), BF),
            pltpu.VMEM((SHARED, BLOCK, HEAD_DIM), BF),
            pltpu.VMEM((KEYS, HEAD_DIM), BF),
            pltpu.VMEM((KEYS, HEAD_DIM), BF),
            pltpu.VMEM((N_DP * UNIT, STEP), BF),
            pltpu.VMEM((N_DP * N_T, STEP), BF),
            pltpu.VMEM((STEP, STEP), BF),
            pltpu.VMEM((STEP, N_DP * UNIT), BF),
            *[pltpu.VMEM((N_DP, UNIT, w), BF) for w in widths],
            *[pltpu.VMEM((N_DP, UNIT, w), BF) for w in widths],
            *[pltpu.VMEM((N_T, UNITS_DEV, w), BF) for w in widths],
            *[pltpu.VMEM((N_T, UNITS_DEV, w), BF) for w in widths],
            dma, dma, dma, dma, dma((3,)), dma((3,)), dma, dma,
            dma((N_CH,)), dma((N_CH,)), dma((N_CH,)), dma((N_CH,)), dma((7,)),
        ],
        compiler_params=pltpu.CompilerParams(
            collective_id=0, has_side_effects=True, vmem_limit_bytes=40 << 20
        ),
    )(
        *[
            pltpu.with_memory_space_constraint(a, pltpu.HBM)
            for a in (
                queries, branch_keys, branch_values, shared_keys, shared_values, ancestry,
                plan.reshape(16, 128),
            )
        ]
    )
    return rows.reshape(UNITS_DEV, 1, HEADS * HEAD_DIM)


def solution(mesh):
    return jax.shard_map(
        body,
        mesh=mesh,
        in_specs=(
            P("dp", "tensor"),
            P("dp", "tensor"),
            P("dp", "tensor"),
            P("dp", "tensor"),
            P("dp", "tensor"),
            P(),
            P(),
        ),
        out_specs=P("dp", "tensor", None),
        check_vma=False,
    )
```

```python
import math

import jax
import jax.numpy as jnp
from jax import lax
from jax.experimental import pallas as pl
from jax.experimental.pallas import tpu as pltpu
from jax.sharding import PartitionSpec as P

HEADS = 40
KV_HEADS = 8
HEAD_DIM = 128
STEP = 256
BLOCK = 64
UNIT = 8
UNITS_DEV = STEP // UNIT
SHARED = 64
MOST = 12
N_DP = 64
N_X = 4
N_Z = 16
N_T = 8
PER = HEADS // KV_HEADS
CHUNKS = (2, 3)
N_CH = len(CHUNKS)
KEYS = STEP + MOST * BLOCK
SCALE = math.log2(math.e) / math.sqrt(HEAD_DIM)
FILL = -1e30
MESH = pl.DeviceIdType.MESH
BF = jnp.bfloat16
F32 = jnp.float32


def iota(shape, dim):
    return lax.broadcasted_iota(jnp.int32, shape, dim)


def dot(a, b, contract=((1,), (0,))):
    return lax.dot_general(a, b, (contract, ((), ())), preferred_element_type=F32)


def flag(mask):
    return jnp.where(mask, 1.0, 0.0).astype(BF)


def kernel(
    q_in, bk_in, bv_in, sk, sv, anc_in, plan_in, out,
    q, anc, plan, kbuf, vbuf, kcat, vcat, pack, pack_row, by_row, pick, *rest
):
    snd, rest = rest[:N_CH], rest[N_CH:]
    rcv, rest = rest[:N_CH], rest[N_CH:]
    tsnd, rest = rest[:N_CH], rest[N_CH:]
    trcv, rest = rest[:N_CH], rest[N_CH:]
    send_k, send_v, got_ka, got_va, got_kb, got_vc, got_kc, got_vb, a_send, a_got, t_send, t_got, load = rest

    dp = lax.axis_index("dp")
    t = lax.axis_index("tensor")
    z, x = dp >> 2, dp & 3

    def at(dz, dx):
        return (((z + dz) & (N_Z - 1)) << 2) + ((x + dx) & (N_X - 1))

    far = [at(4 * i, 0) for i in (1, 2, 3)]
    near = [at(d, 0) for d in (1, -1, 2, -2)]
    side = [at(0, i) for i in (1, 2, 3)]

    def k_at(c, i, count):
        return kbuf.at[pl.ds(x * 16 + c * 4 + i, count)]

    def v_at(c, bx, i, count):
        return vbuf.at[pl.ds(c * 16 + bx * 4 + i, count)]

    k_own, v_own = x * 16, x * 4
    loads = [
        pltpu.make_async_copy(src, dst, load.at[i])
        for i, (src, dst) in enumerate((
            (sk, kbuf.at[k_own]), (sv, vbuf.at[v_own]), (anc_in, anc), (plan_in, plan),
            (q_in, q), (bk_in, kcat.at[pl.ds(0, STEP)]), (bv_in, vcat.at[pl.ds(0, STEP)]),
        ))
    ]
    for copy in loads[:2]:
        copy.start()

    barrier = pltpu.get_barrier_semaphore()
    for peer in far + near + side:
        pl.semaphore_signal(barrier, inc=1, device_id=(peer, t), device_id_type=MESH)
    for i in range(1, N_T):
        pl.semaphore_signal(
            barrier, inc=1, device_id=(dp, (t + i) & (N_T - 1)), device_id_type=MESH
        )
    for copy in loads[2:]:
        copy.start()
    pl.semaphore_wait(barrier, len(far) + len(near) + len(side) + N_T - 1)

    def put(src, dst, send, got, peer):
        pltpu.make_async_remote_copy(
            src_ref=src, dst_ref=dst, send_sem=send, recv_sem=got,
            device_id=(peer, t), device_id_type=MESH,
        ).start()

    def await_blocks(buf, count, sem):
        view = buf.at[pl.ds(0, count)]
        pltpu.make_async_copy(view, view, sem).wait()

    def k_side(c, i, count):
        for peer in side:
            put(k_at(c, i, count), k_at(c, i, count), send_k, got_kc, peer)

    def v_side(i, count, got):
        for n, peer in enumerate(side):
            put(v_at(0, x, i, count), v_at(0, x, i, count), send_v, got.at[n], peer)

    def v_near(bx, i, count):
        block = v_at(0, bx, i, count)
        put(block, v_at(1, bx, i, count), send_v, got_vb, near[0])
        put(block, v_at(2, bx, i, count), send_v, got_vb, near[1])
        third = jnp.where((bx & 1) == 1, near[3], near[2])
        put(block, v_at(3, bx, i, count), send_v, got_vb, third)

    order = (1, 0, 2)
    loads[0].wait()
    for n in order:
        put(kbuf.at[k_own], kbuf.at[k_own + 3 - n], send_k, got_ka, far[n])
    loads[1].wait()
    for n in order:
        put(vbuf.at[v_own], vbuf.at[v_own + 3 - n], send_v, got_va, far[n])
    for n in (0, 1, 2):
        put(k_at(0, 0, 1), k_at(n + 1, 0, 1), send_k, got_kb.at[0, n], near[n])
    v_side(0, 1, got_vc.at[0])
    k_side(0, 0, 1)
    v_near(x, 0, 1)

    for copy in loads[2:]:
        copy.wait()

    def scan(s, carry):
        count, ids = carry
        hit = anc[dp, s] > 0
        ids = tuple(
            jnp.where(jnp.logical_and(hit, count == k), s, ids[k]) for k in range(MOST)
        )
        return count + jnp.where(hit, 1, 0), ids

    zero = jnp.int32(0)
    count, ids = lax.fori_loop(0, SHARED, scan, (zero, (zero,) * MOST))

    rows16 = flag(iota((N_DP, 16), 1) == (iota((N_DP, 16), 0) >> 2))
    spread = dot(rows16, plan[...].astype(F32).astype(BF))
    quarter = (iota((N_DP, 128), 1) >> 5) == (iota((N_DP, 128), 0) & 3)
    fold = flag((iota((128, UNITS_DEV), 0) & 31) == iota((128, UNITS_DEV), 1))
    table = dot(jnp.where(quarter, spread, 0.0).astype(BF), fold)
    widen = flag((iota((UNITS_DEV, STEP), 1) >> 3) == iota((UNITS_DEV, STEP), 0))
    dest = dot(table.astype(BF), widen)
    mine = jnp.sum(jnp.where(iota((N_DP, STEP), 0) == dp, dest, 0.0), axis=0, keepdims=True)
    row_code = mine.astype(jnp.int32) * UNIT + (iota((1, STEP), 1) & 7)
    pack[...] = flag(iota((N_DP * UNIT, STEP), 0) == row_code)
    unit_of = flag((iota((UNITS_DEV, STEP), 1) & 31) == iota((UNITS_DEV, STEP), 0))
    dest = dot(table.astype(BF), unit_of)
    mine = jnp.sum(jnp.where(iota((N_DP, STEP), 0) == dp, dest, 0.0), axis=0, keepdims=True)
    row_code = mine.astype(jnp.int32) * N_T + (iota((1, STEP), 1) >> 5)
    pack_row[...] = flag(iota((N_DP * N_T, STEP), 0) == row_code)
    row, col = iota((STEP, STEP), 0), iota((STEP, STEP), 1)
    by_row[...] = flag((row & 31) * UNIT + (row >> 5) == col)
    to_me = flag(table == dp.astype(F32))
    source = dot(unit_of, to_me, ((0,), (1,)))
    widen_dp = flag((iota((N_DP, N_DP * UNIT), 1) >> 3) == iota((N_DP, N_DP * UNIT), 0))
    source = dot(source.astype(BF), widen_dp)
    same_row = (iota((STEP, N_DP * UNIT), 0) >> 5) == (iota((STEP, N_DP * UNIT), 1) & 7)
    pick[...] = jnp.where(same_row, source, 0.0).astype(BF)

    def forward(r, i, count):
        for n in (0, 1, 2):
            await_blocks(kbuf, count, got_kb.at[r, n])
            k_side(n + 1, i, count)
        for n in (0, 1, 2):
            await_blocks(vbuf, count, got_vc.at[r, n])
            v_near((x + 3 - n) & 3, i, count)

    forward(0, 0, 1)

    await_blocks(kbuf, 3, got_ka)
    put(k_at(0, 1, 3), k_at(1, 1, 3), send_k, got_kb.at[1, 0], near[0])
    put(k_at(0, 1, 3), k_at(2, 1, 3), send_k, got_kb.at[1, 1], near[1])
    put(k_at(0, 1, 1), k_at(3, 1, 1), send_k, got_kb.at[1, 2], near[2])
    put(k_at(0, 1, 2), k_at(3, 2, 2), send_k, got_kb.at[1, 2], near[3])
    await_blocks(vbuf, 3, got_va)
    v_side(1, 3, got_vc.at[1])
    k_side(0, 1, 3)
    v_near(x, 1, 3)
    forward(1, 1, 3)

    def place(s, values):
        bx, away = s & 3, ((s >> 2) - z) & (N_Z - 1)
        low = away & 3
        c = jnp.where(low == 0, 0, jnp.where(low == 1, 2, jnp.where(low == 2, 3, 1)))
        two = jnp.where((bx & 1) == 1, 0, 2) if values else 2
        more = jnp.where(low == 3, 1, jnp.where(low == 2, two, 0))
        i = ((away + more) >> 2) & 3
        return c * 16 + bx * 4 + i if values else bx * 16 + c * 4 + i

    await_blocks(kbuf, 48, got_kc)
    for k in range(MOST):
        kcat[pl.ds(STEP + k * BLOCK, BLOCK), :] = kbuf[place(ids[k], False)]
    await_blocks(vbuf, 48, got_vb)
    for k in range(MOST):
        vcat[pl.ds(STEP + k * BLOCK, BLOCK), :] = vbuf[place(ids[k], True)]

    col = iota((1, KEYS), 1)
    bias = jnp.where(col < STEP + count * BLOCK, 0.0, FILL)
    causal = iota((STEP, STEP), 1) <= iota((STEP, STEP), 0)

    def attend(head):
        qh = q[:, pl.ds(head * HEAD_DIM, HEAD_DIM)]
        scores = dot(qh, kcat[...], ((1,), (1,)))
        local = jnp.where(causal, scores[:, :STEP], FILL)
        shared = scores[:, STEP:] + bias[:, STEP:]
        top = jnp.maximum(
            jnp.max(local, axis=1, keepdims=True), jnp.max(shared, axis=1, keepdims=True)
        )
        local = jnp.exp2((local - top) * SCALE)
        shared = jnp.exp2((shared - top) * SCALE)
        total = jnp.sum(local, axis=1, keepdims=True) + jnp.sum(shared, axis=1, keepdims=True)
        acc = dot(local.astype(BF), vcat[pl.ds(0, STEP), :]) + dot(
            shared.astype(BF), vcat[pl.ds(STEP, MOST * BLOCK), :]
        )
        return (acc / total).astype(BF)

    def send_dp(c):
        def send_one(i, carry):
            m = i >> 2
            half = (m + 1) >> 1
            pz = jnp.where((m & 1) == 1, half, (N_Z - half) & (N_Z - 1))
            peer = (pz << 2) + ((i + x) & (N_X - 1))

            @pl.when(peer != dp)
            def _():
                put(snd[c].at[peer], rcv[c].at[dp], a_send.at[c], a_got.at[c], peer)

            return carry

        lax.fori_loop(0, N_DP, send_one, 0)
        rcv[c][dp] = snd[c][dp]

    def send_tensor(c):
        for i in range(1, N_T):
            peer = (t + i) & (N_T - 1)
            pltpu.make_async_remote_copy(
                src_ref=tsnd[c].at[peer], dst_ref=trcv[c].at[t],
                send_sem=t_send.at[c], recv_sem=t_got.at[c],
                device_id=(dp, peer), device_id_type=MESH,
            ).start()
        trcv[c][t] = tsnd[c][t]

    def picked(c):
        await_blocks(rcv[c], N_DP - 1, a_got.at[c])
        slots = rcv[c][...].reshape(N_DP * UNIT, CHUNKS[c] * HEAD_DIM)
        return dot(pick[...], slots).astype(BF)

    last = N_CH - 1
    head = 0
    for c, heads in enumerate(CHUNKS):
        for h in range(heads):
            merged = attend(head)
            head += 1
            place = pl.ds(h * HEAD_DIM, HEAD_DIM)
            if c < last:
                slots = dot(pack[...], merged).astype(BF)
                snd[c][:, :, place] = slots.reshape(N_DP, UNIT, HEAD_DIM)
            else:
                rows = dot(by_row[...], merged).astype(BF)
                tsnd[c][:, :, place] = rows.reshape(N_T, UNITS_DEV, HEAD_DIM)
        if c < last:
            send_dp(c)
        else:
            send_tensor(c)
    await_blocks(trcv[last], N_T - 1, t_got.at[last])
    wide = CHUNKS[last] * HEAD_DIM
    slots = dot(pack_row[...], trcv[last][...].reshape(STEP, wide)).astype(BF)
    snd[last][...] = slots.reshape(N_DP, N_T, wide)
    send_dp(last)

    for c in range(last):
        tsnd[c][...] = picked(c).reshape(N_T, UNITS_DEV, CHUNKS[c] * HEAD_DIM)
        send_tensor(c)
    start = 0
    for c, heads in enumerate(CHUNKS):
        wide = heads * HEAD_DIM
        if c < last:
            await_blocks(trcv[c], N_T - 1, t_got.at[c])
        else:
            rows = picked(c)
        for peer in range(N_T):
            part = trcv[c][peer] if c < last else rows[peer * UNITS_DEV : (peer + 1) * UNITS_DEV]
            out[:, pl.ds(peer * PER * HEAD_DIM + start, wide)] = part
        start += wide

    await_blocks(kbuf, 63, send_k)
    await_blocks(vbuf, 63, send_v)
    for c in range(N_CH):
        await_blocks(snd[c], N_DP - 1, a_send.at[c])
        await_blocks(tsnd[c], N_T - 1, t_send.at[c])


def body(queries, branch_keys, branch_values, shared_keys, shared_values, ancestry, plan):
    vmem = pl.BlockSpec(memory_space=pltpu.VMEM)
    hbm = pl.BlockSpec(memory_space=pltpu.HBM)
    widths = [heads * HEAD_DIM for heads in CHUNKS]
    dma = pltpu.SemaphoreType.DMA
    rows = pl.pallas_call(
        kernel,
        name="tree_step",
        out_shape=pltpu.VMEM((UNITS_DEV, HEADS * HEAD_DIM), BF),
        in_specs=[hbm] * 7,
        out_specs=vmem,
        scratch_shapes=[
            pltpu.VMEM((STEP, PER * HEAD_DIM), BF),
            pltpu.SMEM((N_DP, SHARED), jnp.int32),
            pltpu.VMEM((16, 128), jnp.int32),
            pltpu.VMEM((SHARED, BLOCK, HEAD_DIM), BF),
            pltpu.VMEM((SHARED, BLOCK, HEAD_DIM), BF),
            pltpu.VMEM((KEYS, HEAD_DIM), BF),
            pltpu.VMEM((KEYS, HEAD_DIM), BF),
            pltpu.VMEM((N_DP * UNIT, STEP), BF),
            pltpu.VMEM((N_DP * N_T, STEP), BF),
            pltpu.VMEM((STEP, STEP), BF),
            pltpu.VMEM((STEP, N_DP * UNIT), BF),
            *[pltpu.VMEM((N_DP, UNIT, w), BF) for w in widths],
            *[pltpu.VMEM((N_DP, UNIT, w), BF) for w in widths],
            *[pltpu.VMEM((N_T, UNITS_DEV, w), BF) for w in widths],
            *[pltpu.VMEM((N_T, UNITS_DEV, w), BF) for w in widths],
            dma, dma, dma, dma, dma((2, 3)), dma((2, 3)), dma, dma,
            dma((N_CH,)), dma((N_CH,)), dma((N_CH,)), dma((N_CH,)), dma((7,)),
        ],
        compiler_params=pltpu.CompilerParams(
            collective_id=0, has_side_effects=True, vmem_limit_bytes=40 << 20
        ),
    )(
        *[
            pltpu.with_memory_space_constraint(a, pltpu.HBM)
            for a in (
                queries, branch_keys, branch_values, shared_keys, shared_values, ancestry,
                plan.reshape(16, 128),
            )
        ]
    )
    return rows.reshape(UNITS_DEV, 1, HEADS * HEAD_DIM)


def solution(mesh):
    return jax.shard_map(
        body,
        mesh=mesh,
        in_specs=(
            P("dp", "tensor"),
            P("dp", "tensor"),
            P("dp", "tensor"),
            P("dp", "tensor"),
            P("dp", "tensor"),
            P(),
            P(),
        ),
        out_specs=P("dp", "tensor", None),
        check_vma=False,
    )
```

```python
import math

import jax
import jax.numpy as jnp
from jax import lax
from jax.experimental import pallas as pl
from jax.experimental.pallas import tpu as pltpu
from jax.sharding import PartitionSpec as P

HEADS = 40
KV_HEADS = 8
HEAD_DIM = 128
STEP = 256
BLOCK = 64
UNIT = 8
UNITS_DEV = STEP // UNIT
SHARED = 64
MOST = 12
N_DP = 64
N_X = 4
N_Z = 16
N_T = 8
PER = HEADS // KV_HEADS
CHUNKS = (2, 3)
N_CH = len(CHUNKS)
KEYS = STEP + MOST * BLOCK
SCALE = math.log2(math.e) / math.sqrt(HEAD_DIM)
FILL = -1e30
MESH = pl.DeviceIdType.MESH
BF = jnp.bfloat16
F32 = jnp.float32


def iota(shape, dim):
    return lax.broadcasted_iota(jnp.int32, shape, dim)


def dot(a, b, contract=((1,), (0,))):
    return lax.dot_general(a, b, (contract, ((), ())), preferred_element_type=F32)


def flag(mask):
    return jnp.where(mask, 1.0, 0.0).astype(BF)


def kernel(
    q_in, bk_in, bv_in, sk, sv, anc_in, plan_in, out,
    q, anc, plan, kbuf, vbuf, kcat, vcat, weights, pack, pack_row, by_row, pick, *rest
):
    snd, rest = rest[:N_CH], rest[N_CH:]
    rcv, rest = rest[:N_CH], rest[N_CH:]
    tsnd, rest = rest[:N_CH], rest[N_CH:]
    trcv, rest = rest[:N_CH], rest[N_CH:]
    send_k, send_v, got_ka, got_va, got_kb, got_vc, got_kc, got_vb, a_send, a_got, t_send, t_got, load = rest

    dp = lax.axis_index("dp")
    t = lax.axis_index("tensor")
    z, x = dp >> 2, dp & 3

    def at(dz, dx):
        return (((z + dz) & (N_Z - 1)) << 2) + ((x + dx) & (N_X - 1))

    far = [at(4 * i, 0) for i in (1, 2, 3)]
    near = [at(d, 0) for d in (1, -1, 2, -2)]
    side = [at(0, i) for i in (1, 2, 3)]

    def k_at(c, i, count):
        return kbuf.at[pl.ds(x * 16 + c * 4 + i, count)]

    def v_at(c, bx, i, count):
        return vbuf.at[pl.ds(c * 16 + bx * 4 + i, count)]

    k_own, v_own = x * 16, x * 4
    loads = [
        pltpu.make_async_copy(src, dst, load.at[i])
        for i, (src, dst) in enumerate((
            (sk, kbuf.at[k_own]), (sv, vbuf.at[v_own]), (anc_in, anc), (plan_in, plan),
            (q_in, q), (bk_in, kcat.at[pl.ds(0, STEP)]), (bv_in, vcat.at[pl.ds(0, STEP)]),
        ))
    ]
    for copy in loads[:2]:
        copy.start()

    barrier = pltpu.get_barrier_semaphore()
    for peer in far + near + side:
        pl.semaphore_signal(barrier, inc=1, device_id=(peer, t), device_id_type=MESH)
    for i in range(1, N_T):
        pl.semaphore_signal(
            barrier, inc=1, device_id=(dp, (t + i) & (N_T - 1)), device_id_type=MESH
        )
    for copy in loads[2:]:
        copy.start()
    pl.semaphore_wait(barrier, len(far) + len(near) + len(side) + N_T - 1)

    def put(src, dst, send, got, peer):
        pltpu.make_async_remote_copy(
            src_ref=src, dst_ref=dst, send_sem=send, recv_sem=got,
            device_id=(peer, t), device_id_type=MESH,
        ).start()

    def await_blocks(buf, count, sem):
        view = buf.at[pl.ds(0, count)]
        pltpu.make_async_copy(view, view, sem).wait()

    def k_side(c, i, count):
        for peer in side:
            put(k_at(c, i, count), k_at(c, i, count), send_k, got_kc, peer)

    def v_side(i, count, got):
        for n, peer in enumerate(side):
            put(v_at(0, x, i, count), v_at(0, x, i, count), send_v, got.at[n], peer)

    def v_near(bx, i, count):
        block = v_at(0, bx, i, count)
        put(block, v_at(1, bx, i, count), send_v, got_vb, near[0])
        put(block, v_at(2, bx, i, count), send_v, got_vb, near[1])
        third = jnp.where((bx & 1) == 1, near[3], near[2])
        put(block, v_at(3, bx, i, count), send_v, got_vb, third)

    order = (1, 0, 2)
    loads[0].wait()
    for n in order:
        put(kbuf.at[k_own], kbuf.at[k_own + 3 - n], send_k, got_ka, far[n])
    loads[1].wait()
    for n in order:
        put(vbuf.at[v_own], vbuf.at[v_own + 3 - n], send_v, got_va, far[n])
    for n in (0, 1, 2):
        put(k_at(0, 0, 1), k_at(n + 1, 0, 1), send_k, got_kb.at[0, n], near[n])
    v_side(0, 1, got_vc.at[0])
    k_side(0, 0, 1)
    v_near(x, 0, 1)

    for copy in loads[2:]:
        copy.wait()

    def scan(s, carry):
        count, ids = carry
        hit = anc[dp, s] > 0
        ids = tuple(
            jnp.where(jnp.logical_and(hit, count == k), s, ids[k]) for k in range(MOST)
        )
        return count + jnp.where(hit, 1, 0), ids

    zero = jnp.int32(0)
    count, ids = lax.fori_loop(0, SHARED, scan, (zero, (zero,) * MOST))

    rows16 = flag(iota((N_DP, 16), 1) == (iota((N_DP, 16), 0) >> 2))
    spread = dot(rows16, plan[...].astype(F32).astype(BF))
    quarter = (iota((N_DP, 128), 1) >> 5) == (iota((N_DP, 128), 0) & 3)
    fold = flag((iota((128, UNITS_DEV), 0) & 31) == iota((128, UNITS_DEV), 1))
    table = dot(jnp.where(quarter, spread, 0.0).astype(BF), fold)
    widen = flag((iota((UNITS_DEV, STEP), 1) >> 3) == iota((UNITS_DEV, STEP), 0))
    dest = dot(table.astype(BF), widen)
    mine = jnp.sum(jnp.where(iota((N_DP, STEP), 0) == dp, dest, 0.0), axis=0, keepdims=True)
    row_code = mine.astype(jnp.int32) * UNIT + (iota((1, STEP), 1) & 7)
    pack[...] = flag(iota((N_DP * UNIT, STEP), 0) == row_code)
    unit_of = flag((iota((UNITS_DEV, STEP), 1) & 31) == iota((UNITS_DEV, STEP), 0))
    dest = dot(table.astype(BF), unit_of)
    mine = jnp.sum(jnp.where(iota((N_DP, STEP), 0) == dp, dest, 0.0), axis=0, keepdims=True)
    row_code = mine.astype(jnp.int32) * N_T + (iota((1, STEP), 1) >> 5)
    pack_row[...] = flag(iota((N_DP * N_T, STEP), 0) == row_code)
    row, col = iota((STEP, STEP), 0), iota((STEP, STEP), 1)
    by_row[...] = flag((row & 31) * UNIT + (row >> 5) == col)
    to_me = flag(table == dp.astype(F32))
    source = dot(unit_of, to_me, ((0,), (1,)))
    widen_dp = flag((iota((N_DP, N_DP * UNIT), 1) >> 3) == iota((N_DP, N_DP * UNIT), 0))
    source = dot(source.astype(BF), widen_dp)
    same_row = (iota((STEP, N_DP * UNIT), 0) >> 5) == (iota((STEP, N_DP * UNIT), 1) & 7)
    pick[...] = jnp.where(same_row, source, 0.0).astype(BF)

    def forward(r, i, count):
        for n in (0, 1, 2):
            await_blocks(kbuf, count, got_kb.at[r, n])
            k_side(n + 1, i, count)
        for n in (0, 1, 2):
            await_blocks(vbuf, count, got_vc.at[r, n])
            v_near((x + 3 - n) & 3, i, count)

    forward(0, 0, 1)

    await_blocks(kbuf, 3, got_ka)
    put(k_at(0, 1, 3), k_at(1, 1, 3), send_k, got_kb.at[1, 0], near[0])
    put(k_at(0, 1, 3), k_at(2, 1, 3), send_k, got_kb.at[1, 1], near[1])
    put(k_at(0, 1, 1), k_at(3, 1, 1), send_k, got_kb.at[1, 2], near[2])
    put(k_at(0, 1, 2), k_at(3, 2, 2), send_k, got_kb.at[1, 2], near[3])
    await_blocks(vbuf, 3, got_va)
    v_side(1, 3, got_vc.at[1])
    k_side(0, 1, 3)
    v_near(x, 1, 3)
    forward(1, 1, 3)

    def place(s, values):
        bx, away = s & 3, ((s >> 2) - z) & (N_Z - 1)
        low = away & 3
        c = jnp.where(low == 0, 0, jnp.where(low == 1, 2, jnp.where(low == 2, 3, 1)))
        two = jnp.where((bx & 1) == 1, 0, 2) if values else 2
        more = jnp.where(low == 3, 1, jnp.where(low == 2, two, 0))
        i = ((away + more) >> 2) & 3
        return c * 16 + bx * 4 + i if values else bx * 16 + c * 4 + i

    await_blocks(kbuf, 48, got_kc)
    for k in range(MOST):
        kcat[pl.ds(STEP + k * BLOCK, BLOCK), :] = kbuf[place(ids[k], False)]
    col = iota((1, KEYS), 1)
    bias = jnp.where(col < STEP + count * BLOCK, 0.0, FILL)
    causal = iota((STEP, STEP), 1) <= iota((STEP, STEP), 0)

    def weigh(head):
        qh = q[:, pl.ds(head * HEAD_DIM, HEAD_DIM)]
        scores = dot(qh, kcat[...], ((1,), (1,)))
        local = jnp.where(causal, scores[:, :STEP], FILL)
        shared = scores[:, STEP:] + bias[:, STEP:]
        top = jnp.maximum(
            jnp.max(local, axis=1, keepdims=True), jnp.max(shared, axis=1, keepdims=True)
        )
        local = jnp.exp2((local - top) * SCALE)
        shared = jnp.exp2((shared - top) * SCALE)
        total = jnp.sum(local, axis=1, keepdims=True) + jnp.sum(shared, axis=1, keepdims=True)
        return local.astype(BF), shared.astype(BF), total

    totals = []
    for head in range(CHUNKS[0]):
        local, shared, total = weigh(head)
        weights[head, :, pl.ds(0, STEP)] = local
        weights[head, :, pl.ds(STEP, MOST * BLOCK)] = shared
        totals.append(total)

    await_blocks(vbuf, 48, got_vb)
    for k in range(MOST):
        vcat[pl.ds(STEP + k * BLOCK, BLOCK), :] = vbuf[place(ids[k], True)]

    def attend(head):
        if head < CHUNKS[0]:
            return (dot(weights[head], vcat[...]) / totals[head]).astype(BF)
        local, shared, total = weigh(head)
        acc = dot(local, vcat[pl.ds(0, STEP), :]) + dot(
            shared, vcat[pl.ds(STEP, MOST * BLOCK), :]
        )
        return (acc / total).astype(BF)

    def send_dp(c, low, high):
        def send_one(i, carry):
            m = i >> 2
            half = (m + 1) >> 1
            pz = jnp.where((m & 1) == 1, half, (N_Z - half) & (N_Z - 1))
            peer = (pz << 2) + ((i + x) & (N_X - 1))

            @pl.when(peer != dp)
            def _():
                put(snd[c].at[peer], rcv[c].at[dp], a_send.at[c], a_got.at[c], peer)

            return carry

        lax.fori_loop(low, high, send_one, 0)

    def send_tensor(c):
        for i in range(1, N_T):
            peer = (t + i) & (N_T - 1)
            pltpu.make_async_remote_copy(
                src_ref=tsnd[c].at[peer], dst_ref=trcv[c].at[t],
                send_sem=t_send.at[c], recv_sem=t_got.at[c],
                device_id=(dp, peer), device_id_type=MESH,
            ).start()
        trcv[c][t] = tsnd[c][t]

    def picked(c):
        await_blocks(rcv[c], N_DP - 1, a_got.at[c])
        slots = rcv[c][...].reshape(N_DP * UNIT, CHUNKS[c] * HEAD_DIM)
        return dot(pick[...], slots).astype(BF)

    last = N_CH - 1
    head = 0
    for c, heads in enumerate(CHUNKS):
        for h in range(heads):
            merged = attend(head)
            head += 1
            place = pl.ds(h * HEAD_DIM, HEAD_DIM)
            if c < last:
                slots = dot(pack[...], merged).astype(BF)
                snd[c][:, :, place] = slots.reshape(N_DP, UNIT, HEAD_DIM)
            else:
                rows = dot(by_row[...], merged).astype(BF)
                tsnd[c][:, :, place] = rows.reshape(N_T, UNITS_DEV, HEAD_DIM)
        if c < last:
            send_dp(c, 0, 32)
        else:
            send_tensor(c)
            for before in range(last):
                send_dp(before, 32, N_DP)
    await_blocks(trcv[last], N_T - 1, t_got.at[last])
    wide = CHUNKS[last] * HEAD_DIM
    slots = dot(pack_row[...], trcv[last][...].reshape(STEP, wide)).astype(BF)
    snd[last][...] = slots.reshape(N_DP, N_T, wide)
    send_dp(last, 0, N_DP)
    for c in range(N_CH):
        rcv[c][dp] = snd[c][dp]

    for c in range(last):
        tsnd[c][...] = picked(c).reshape(N_T, UNITS_DEV, CHUNKS[c] * HEAD_DIM)
        send_tensor(c)
    start = 0
    for c, heads in enumerate(CHUNKS):
        wide = heads * HEAD_DIM
        if c < last:
            await_blocks(trcv[c], N_T - 1, t_got.at[c])
        else:
            rows = picked(c)
        for peer in range(N_T):
            part = trcv[c][peer] if c < last else rows[peer * UNITS_DEV : (peer + 1) * UNITS_DEV]
            out[:, pl.ds(peer * PER * HEAD_DIM + start, wide)] = part
        start += wide

    await_blocks(kbuf, 63, send_k)
    await_blocks(vbuf, 63, send_v)
    for c in range(N_CH):
        await_blocks(snd[c], N_DP - 1, a_send.at[c])
        await_blocks(tsnd[c], N_T - 1, t_send.at[c])


def body(queries, branch_keys, branch_values, shared_keys, shared_values, ancestry, plan):
    vmem = pl.BlockSpec(memory_space=pltpu.VMEM)
    hbm = pl.BlockSpec(memory_space=pltpu.HBM)
    widths = [heads * HEAD_DIM for heads in CHUNKS]
    dma = pltpu.SemaphoreType.DMA
    rows = pl.pallas_call(
        kernel,
        name="tree_step",
        out_shape=pltpu.VMEM((UNITS_DEV, HEADS * HEAD_DIM), BF),
        in_specs=[hbm] * 7,
        out_specs=vmem,
        scratch_shapes=[
            pltpu.VMEM((STEP, PER * HEAD_DIM), BF),
            pltpu.SMEM((N_DP, SHARED), jnp.int32),
            pltpu.VMEM((16, 128), jnp.int32),
            pltpu.VMEM((SHARED, BLOCK, HEAD_DIM), BF),
            pltpu.VMEM((SHARED, BLOCK, HEAD_DIM), BF),
            pltpu.VMEM((KEYS, HEAD_DIM), BF),
            pltpu.VMEM((KEYS, HEAD_DIM), BF),
            pltpu.VMEM((CHUNKS[0], STEP, KEYS), BF),
            pltpu.VMEM((N_DP * UNIT, STEP), BF),
            pltpu.VMEM((N_DP * N_T, STEP), BF),
            pltpu.VMEM((STEP, STEP), BF),
            pltpu.VMEM((STEP, N_DP * UNIT), BF),
            *[pltpu.VMEM((N_DP, UNIT, w), BF) for w in widths],
            *[pltpu.VMEM((N_DP, UNIT, w), BF) for w in widths],
            *[pltpu.VMEM((N_T, UNITS_DEV, w), BF) for w in widths],
            *[pltpu.VMEM((N_T, UNITS_DEV, w), BF) for w in widths],
            dma, dma, dma, dma, dma((2, 3)), dma((2, 3)), dma, dma,
            dma((N_CH,)), dma((N_CH,)), dma((N_CH,)), dma((N_CH,)), dma((7,)),
        ],
        compiler_params=pltpu.CompilerParams(
            collective_id=0, has_side_effects=True, vmem_limit_bytes=40 << 20
        ),
    )(
        *[
            pltpu.with_memory_space_constraint(a, pltpu.HBM)
            for a in (
                queries, branch_keys, branch_values, shared_keys, shared_values, ancestry,
                plan.reshape(16, 128),
            )
        ]
    )
    return rows.reshape(UNITS_DEV, 1, HEADS * HEAD_DIM)


def solution(mesh):
    return jax.shard_map(
        body,
        mesh=mesh,
        in_specs=(
            P("dp", "tensor"),
            P("dp", "tensor"),
            P("dp", "tensor"),
            P("dp", "tensor"),
            P("dp", "tensor"),
            P(),
            P(),
        ),
        out_specs=P("dp", "tensor", None),
        check_vma=False,
    )
```

```python
import math

import jax
import jax.numpy as jnp
from jax import lax
from jax.experimental import pallas as pl
from jax.experimental.pallas import tpu as pltpu
from jax.sharding import PartitionSpec as P

HEADS = 40
KV_HEADS = 8
HEAD_DIM = 128
STEP = 256
BLOCK = 64
UNIT = 8
UNITS_DEV = STEP // UNIT
SHARED = 64
MOST = 12
N_DP = 64
N_X = 4
N_Z = 16
N_T = 8
PER = HEADS // KV_HEADS
CHUNKS = (2, 3)
N_CH = len(CHUNKS)
KEYS = STEP + MOST * BLOCK
SCALE = math.log2(math.e) / math.sqrt(HEAD_DIM)
FILL = -1e30
MESH = pl.DeviceIdType.MESH
BF = jnp.bfloat16
F32 = jnp.float32


def iota(shape, dim):
    return lax.broadcasted_iota(jnp.int32, shape, dim)


def dot(a, b, contract=((1,), (0,))):
    return lax.dot_general(a, b, (contract, ((), ())), preferred_element_type=F32)


def flag(mask):
    return jnp.where(mask, 1.0, 0.0).astype(BF)


def kernel(
    q_in, bk_in, bv_in, sk, sv, anc_in, plan_in, out,
    q, anc, plan, kbuf, vbuf, kcat, vcat, weights, pack, pack_row, by_row, pick, *rest
):
    snd, rest = rest[:N_CH], rest[N_CH:]
    rcv, rest = rest[:N_CH], rest[N_CH:]
    tsnd, rest = rest[:N_CH], rest[N_CH:]
    trcv, rest = rest[:N_CH], rest[N_CH:]
    send_k, send_v, got_ka, got_va, got_kb, got_vc, got_kc, got_vb, a_send, a_got, t_send, t_got, load = rest

    dp = lax.axis_index("dp")
    t = lax.axis_index("tensor")
    z, x = dp >> 2, dp & 3

    def at(dz, dx):
        return (((z + dz) & (N_Z - 1)) << 2) + ((x + dx) & (N_X - 1))

    far = [at(4 * i, 0) for i in (1, 2, 3)]
    near = [at(d, 0) for d in (1, -1, 2, -2)]
    side = [at(0, i) for i in (1, 2, 3)]

    def k_at(c, i, count):
        return kbuf.at[pl.ds(x * 16 + c * 4 + i, count)]

    def v_at(c, bx, i, count):
        return vbuf.at[pl.ds(c * 16 + bx * 4 + i, count)]

    k_own, v_own = x * 16, x * 4
    loads = [
        pltpu.make_async_copy(src, dst, load.at[i])
        for i, (src, dst) in enumerate((
            (sk, kbuf.at[k_own]), (sv, vbuf.at[v_own]), (anc_in, anc), (plan_in, plan),
            (q_in, q), (bk_in, kcat.at[pl.ds(0, STEP)]), (bv_in, vcat.at[pl.ds(0, STEP)]),
        ))
    ]
    for copy in loads[:2]:
        copy.start()

    barrier = pltpu.get_barrier_semaphore()
    for peer in far + near + side:
        pl.semaphore_signal(barrier, inc=1, device_id=(peer, t), device_id_type=MESH)
    for i in range(1, N_T):
        pl.semaphore_signal(
            barrier, inc=1, device_id=(dp, (t + i) & (N_T - 1)), device_id_type=MESH
        )
    for copy in loads[2:]:
        copy.start()
    pl.semaphore_wait(barrier, len(far) + len(near) + len(side) + N_T - 1)

    def put(src, dst, send, got, peer):
        pltpu.make_async_remote_copy(
            src_ref=src, dst_ref=dst, send_sem=send, recv_sem=got,
            device_id=(peer, t), device_id_type=MESH,
        ).start()

    def await_blocks(buf, count, sem):
        view = buf.at[pl.ds(0, count)]
        pltpu.make_async_copy(view, view, sem).wait()

    def k_side(c, i, count):
        for peer in side:
            put(k_at(c, i, count), k_at(c, i, count), send_k, got_kc, peer)

    def v_side(i, count, got):
        for n, peer in enumerate(side):
            put(v_at(0, x, i, count), v_at(0, x, i, count), send_v, got.at[n], peer)

    def v_near(bx, i, count):
        block = v_at(0, bx, i, count)
        put(block, v_at(1, bx, i, count), send_v, got_vb, near[0])
        put(block, v_at(2, bx, i, count), send_v, got_vb, near[1])
        third = jnp.where((bx & 1) == 1, near[3], near[2])
        put(block, v_at(3, bx, i, count), send_v, got_vb, third)

    order = (1, 0, 2)
    loads[0].wait()
    for n in order:
        put(kbuf.at[k_own], kbuf.at[k_own + 3 - n], send_k, got_ka, far[n])
    loads[1].wait()
    for n in order:
        put(vbuf.at[v_own], vbuf.at[v_own + 3 - n], send_v, got_va, far[n])
    for n in (0, 1, 2):
        put(k_at(0, 0, 1), k_at(n + 1, 0, 1), send_k, got_kb.at[0, n], near[n])
    v_side(0, 1, got_vc.at[0])
    k_side(0, 0, 1)
    v_near(x, 0, 1)

    for copy in loads[2:]:
        copy.wait()

    def scan(s, carry):
        count, ids = carry
        hit = anc[dp, s] > 0
        ids = tuple(
            jnp.where(jnp.logical_and(hit, count == k), s, ids[k]) for k in range(MOST)
        )
        return count + jnp.where(hit, 1, 0), ids

    zero = jnp.int32(0)
    count, ids = lax.fori_loop(0, SHARED, scan, (zero, (zero,) * MOST))

    rows16 = flag(iota((N_DP, 16), 1) == (iota((N_DP, 16), 0) >> 2))
    spread = dot(rows16, plan[...].astype(F32).astype(BF))
    quarter = (iota((N_DP, 128), 1) >> 5) == (iota((N_DP, 128), 0) & 3)
    fold = flag((iota((128, UNITS_DEV), 0) & 31) == iota((128, UNITS_DEV), 1))
    table = dot(jnp.where(quarter, spread, 0.0).astype(BF), fold)
    widen = flag((iota((UNITS_DEV, STEP), 1) >> 3) == iota((UNITS_DEV, STEP), 0))
    dest = dot(table.astype(BF), widen)
    mine = jnp.sum(jnp.where(iota((N_DP, STEP), 0) == dp, dest, 0.0), axis=0, keepdims=True)
    row_code = mine.astype(jnp.int32) * UNIT + (iota((1, STEP), 1) & 7)
    pack[...] = flag(iota((N_DP * UNIT, STEP), 0) == row_code)
    unit_of = flag((iota((UNITS_DEV, STEP), 1) & 31) == iota((UNITS_DEV, STEP), 0))
    dest = dot(table.astype(BF), unit_of)
    mine = jnp.sum(jnp.where(iota((N_DP, STEP), 0) == dp, dest, 0.0), axis=0, keepdims=True)
    row_code = mine.astype(jnp.int32) * N_T + (iota((1, STEP), 1) >> 5)
    pack_row[...] = flag(iota((N_DP * N_T, STEP), 0) == row_code)
    row, col = iota((STEP, STEP), 0), iota((STEP, STEP), 1)
    by_row[...] = flag((row & 31) * UNIT + (row >> 5) == col)
    to_me = flag(table == dp.astype(F32))
    source = dot(unit_of, to_me, ((0,), (1,)))
    widen_dp = flag((iota((N_DP, N_DP * UNIT), 1) >> 3) == iota((N_DP, N_DP * UNIT), 0))
    source = dot(source.astype(BF), widen_dp)
    same_row = (iota((STEP, N_DP * UNIT), 0) >> 5) == (iota((STEP, N_DP * UNIT), 1) & 7)
    pick[...] = jnp.where(same_row, source, 0.0).astype(BF)

    def forward(r, i, count):
        for k, v in ((0, 0), (1, 2), (2, 1)):
            await_blocks(kbuf, count, got_kb.at[r, k])
            k_side(k + 1, i, count)
            await_blocks(vbuf, count, got_vc.at[r, v])
            v_near((x + 3 - v) & 3, i, count)

    forward(0, 0, 1)

    await_blocks(kbuf, 3, got_ka)
    put(k_at(0, 1, 3), k_at(1, 1, 3), send_k, got_kb.at[1, 0], near[0])
    put(k_at(0, 1, 3), k_at(2, 1, 3), send_k, got_kb.at[1, 1], near[1])
    put(k_at(0, 1, 1), k_at(3, 1, 1), send_k, got_kb.at[1, 2], near[2])
    put(k_at(0, 1, 2), k_at(3, 2, 2), send_k, got_kb.at[1, 2], near[3])
    await_blocks(vbuf, 3, got_va)
    v_side(1, 3, got_vc.at[1])
    k_side(0, 1, 3)
    v_near(x, 1, 3)
    forward(1, 1, 3)

    def place(s, values):
        bx, away = s & 3, ((s >> 2) - z) & (N_Z - 1)
        low = away & 3
        c = jnp.where(low == 0, 0, jnp.where(low == 1, 2, jnp.where(low == 2, 3, 1)))
        two = jnp.where((bx & 1) == 1, 0, 2) if values else 2
        more = jnp.where(low == 3, 1, jnp.where(low == 2, two, 0))
        i = ((away + more) >> 2) & 3
        return c * 16 + bx * 4 + i if values else bx * 16 + c * 4 + i

    await_blocks(kbuf, 48, got_kc)
    for k in range(MOST):
        kcat[pl.ds(STEP + k * BLOCK, BLOCK), :] = kbuf[place(ids[k], False)]
    col = iota((1, KEYS), 1)
    bias = jnp.where(col < STEP + count * BLOCK, 0.0, FILL)
    causal = iota((STEP, STEP), 1) <= iota((STEP, STEP), 0)

    def weigh(head):
        qh = q[:, pl.ds(head * HEAD_DIM, HEAD_DIM)]
        scores = dot(qh, kcat[...], ((1,), (1,)))
        local = jnp.where(causal, scores[:, :STEP], FILL)
        shared = scores[:, STEP:] + bias[:, STEP:]
        top = jnp.maximum(
            jnp.max(local, axis=1, keepdims=True), jnp.max(shared, axis=1, keepdims=True)
        )
        local = jnp.exp2((local - top) * SCALE)
        shared = jnp.exp2((shared - top) * SCALE)
        total = jnp.sum(local, axis=1, keepdims=True) + jnp.sum(shared, axis=1, keepdims=True)
        return local.astype(BF), shared.astype(BF), total

    totals = []
    for head in range(CHUNKS[0]):
        local, shared, total = weigh(head)
        weights[head, :, pl.ds(0, STEP)] = local
        weights[head, :, pl.ds(STEP, MOST * BLOCK)] = shared
        totals.append(total)

    await_blocks(vbuf, 48, got_vb)
    for k in range(MOST):
        vcat[pl.ds(STEP + k * BLOCK, BLOCK), :] = vbuf[place(ids[k], True)]

    def attend(head):
        if head < CHUNKS[0]:
            return (dot(weights[head], vcat[...]) / totals[head]).astype(BF)
        local, shared, total = weigh(head)
        acc = dot(local, vcat[pl.ds(0, STEP), :]) + dot(
            shared, vcat[pl.ds(STEP, MOST * BLOCK), :]
        )
        return (acc / total).astype(BF)

    def send_dp(c, low, high):
        def send_one(i, carry):
            m = i >> 2
            half = (m + 1) >> 1
            pz = jnp.where((m & 1) == 1, half + 1, N_Z + 1 - half)
            pz = jnp.where(m < 3, m, pz)
            peer = (pz << 2) + ((i + x) & (N_X - 1))

            @pl.when(peer != dp)
            def _():
                put(snd[c].at[peer], rcv[c].at[dp], a_send.at[c], a_got.at[c], peer)

            return carry

        lax.fori_loop(low, high, send_one, 0)

    def send_tensor(c):
        for i in range(1, N_T):
            peer = (t + i) & (N_T - 1)
            pltpu.make_async_remote_copy(
                src_ref=tsnd[c].at[peer], dst_ref=trcv[c].at[t],
                send_sem=t_send.at[c], recv_sem=t_got.at[c],
                device_id=(dp, peer), device_id_type=MESH,
            ).start()
        trcv[c][t] = tsnd[c][t]

    def picked(c):
        await_blocks(rcv[c], N_DP - 1, a_got.at[c])
        slots = rcv[c][...].reshape(N_DP * UNIT, CHUNKS[c] * HEAD_DIM)
        return dot(pick[...], slots).astype(BF)

    last = N_CH - 1
    head = 0
    for c, heads in enumerate(CHUNKS):
        for h in range(heads):
            merged = attend(head)
            head += 1
            place = pl.ds(h * HEAD_DIM, HEAD_DIM)
            if c < last:
                slots = dot(pack[...], merged).astype(BF)
                snd[c][:, :, place] = slots.reshape(N_DP, UNIT, HEAD_DIM)
            else:
                rows = dot(by_row[...], merged).astype(BF)
                tsnd[c][:, :, place] = rows.reshape(N_T, UNITS_DEV, HEAD_DIM)
        if c < last:
            send_dp(c, 0, 32)
        else:
            send_tensor(c)
            for before in range(last):
                send_dp(before, 32, N_DP)
    await_blocks(trcv[last], N_T - 1, t_got.at[last])
    wide = CHUNKS[last] * HEAD_DIM
    slots = dot(pack_row[...], trcv[last][...].reshape(STEP, wide)).astype(BF)
    snd[last][...] = slots.reshape(N_DP, N_T, wide)
    send_dp(last, 0, N_DP)
    for c in range(N_CH):
        rcv[c][dp] = snd[c][dp]

    for c in range(last):
        tsnd[c][...] = picked(c).reshape(N_T, UNITS_DEV, CHUNKS[c] * HEAD_DIM)
        send_tensor(c)
    start = 0
    for c, heads in enumerate(CHUNKS):
        wide = heads * HEAD_DIM
        if c < last:
            await_blocks(trcv[c], N_T - 1, t_got.at[c])
        else:
            rows = picked(c)
        for peer in range(N_T):
            part = trcv[c][peer] if c < last else rows[peer * UNITS_DEV : (peer + 1) * UNITS_DEV]
            out[:, pl.ds(peer * PER * HEAD_DIM + start, wide)] = part
        start += wide

    await_blocks(kbuf, 63, send_k)
    await_blocks(vbuf, 63, send_v)
    for c in range(N_CH):
        await_blocks(snd[c], N_DP - 1, a_send.at[c])
        await_blocks(tsnd[c], N_T - 1, t_send.at[c])


def body(queries, branch_keys, branch_values, shared_keys, shared_values, ancestry, plan):
    vmem = pl.BlockSpec(memory_space=pltpu.VMEM)
    hbm = pl.BlockSpec(memory_space=pltpu.HBM)
    widths = [heads * HEAD_DIM for heads in CHUNKS]
    dma = pltpu.SemaphoreType.DMA
    rows = pl.pallas_call(
        kernel,
        name="tree_step",
        out_shape=pltpu.VMEM((UNITS_DEV, HEADS * HEAD_DIM), BF),
        in_specs=[hbm] * 7,
        out_specs=vmem,
        scratch_shapes=[
            pltpu.VMEM((STEP, PER * HEAD_DIM), BF),
            pltpu.SMEM((N_DP, SHARED), jnp.int32),
            pltpu.VMEM((16, 128), jnp.int32),
            pltpu.VMEM((SHARED, BLOCK, HEAD_DIM), BF),
            pltpu.VMEM((SHARED, BLOCK, HEAD_DIM), BF),
            pltpu.VMEM((KEYS, HEAD_DIM), BF),
            pltpu.VMEM((KEYS, HEAD_DIM), BF),
            pltpu.VMEM((CHUNKS[0], STEP, KEYS), BF),
            pltpu.VMEM((N_DP * UNIT, STEP), BF),
            pltpu.VMEM((N_DP * N_T, STEP), BF),
            pltpu.VMEM((STEP, STEP), BF),
            pltpu.VMEM((STEP, N_DP * UNIT), BF),
            *[pltpu.VMEM((N_DP, UNIT, w), BF) for w in widths],
            *[pltpu.VMEM((N_DP, UNIT, w), BF) for w in widths],
            *[pltpu.VMEM((N_T, UNITS_DEV, w), BF) for w in widths],
            *[pltpu.VMEM((N_T, UNITS_DEV, w), BF) for w in widths],
            dma, dma, dma, dma, dma((2, 3)), dma((2, 3)), dma, dma,
            dma((N_CH,)), dma((N_CH,)), dma((N_CH,)), dma((N_CH,)), dma((7,)),
        ],
        compiler_params=pltpu.CompilerParams(
            collective_id=0, has_side_effects=True, vmem_limit_bytes=40 << 20
        ),
    )(
        *[
            pltpu.with_memory_space_constraint(a, pltpu.HBM)
            for a in (
                queries, branch_keys, branch_values, shared_keys, shared_values, ancestry,
                plan.reshape(16, 128),
            )
        ]
    )
    return rows.reshape(UNITS_DEV, 1, HEADS * HEAD_DIM)


def solution(mesh):
    return jax.shard_map(
        body,
        mesh=mesh,
        in_specs=(
            P("dp", "tensor"),
            P("dp", "tensor"),
            P("dp", "tensor"),
            P("dp", "tensor"),
            P("dp", "tensor"),
            P(),
            P(),
        ),
        out_specs=P("dp", "tensor", None),
        check_vma=False,
    )
```
